768 devices in a mesh: gy: 96 (over z, y), gx: 8 (over x, core).
Axes of the slice: x: 4, y: 8, z: 12, core: 2. Of those that a mesh axis runs over, the one named last changes fastest.
Arguments:
- sea_level: float32 [11520, 2048], P('gy', 'gx'), may hold values from -4 to 4
- transport_x: float32 [11520, 2048], P('gy', 'gx'), may hold values from -5 to 5
- transport_y: float32 [11520, 2048], P('gy', 'gx'), may hold values from -5 to 5
- friction: float32 [11520, 2048], P('gy', 'gx'), may hold values from 0.05 to 0.5
- levels: int32 [11520, 2048], P('gy', 'gx'), may hold values from 15 to 60
- strip_map: int32 [11520], P('gy'), may hold values from 0 to 2303, as said below
- parent_strip: float32 [2, 4, 2, 2304], P(None, None, None, ('gy', 'gx')), may hold values from -5 to 5
- plat_tile: int32 [3072], replicated, may hold values from 0 to 767
- plat_row: int32 [3072], replicated, may hold values from 0 to 119
- plat_col: int32 [3072], replicated, may hold values from 0 to 255
- plat_drag: float32 [60, 3072], P(None, ('gy', 'gx')), may hold values from 0.05 to 0.5
- plat_shear: float32 [2, 60, 3072], P(None, None, ('gy', 'gx')), may hold values from -3 to 3
Outputs:
- sea_out: float32 [11520, 2048], P('gy', 'gx')
- flow_x: float32 [11520, 2048], P('gy', 'gx')
- flow_y: float32 [11520, 2048], P('gy', 'gx')
The draws below stay inside these ranges and needn't reach their ends.
Inputs may be any that keep to these rules, and one draw needn't show every extreme that they name: For a child row in row block g (rows g * 120 to g * 120 + 119) strip_map lies within g * 24 - 1 to g * 24 + 24.
All inputs are finite; a program needn't handle non-finite values.
Results may differ from the reference program's by a relative error of at most 0.00002.
Values sent between devices are 32-bit elements; how exact they have to be, the bound alone decides.
No kernel may reach another device: no remote copies, remote signals or barrier semaphores. Data moves between devices by JAX's collectives and lax.ppermute only.
A program may use at most 32 MiB of HBM per device.

```python
import math
import jax
import jax.numpy as jnp
import numpy as np
from jax import lax

CY = 120
CX = 256
SUBSTEPS = 4
LEVELS = 60
RATIO = 5
NY = 11520
NX = 2048
NP = 2304
PLAT = 3072
N_GY = 96
N_GX = 8


def draw_sea_level(key, part):
    normal_draw = jax.random.normal(key, (NY, NX), jnp.float32)
    return jnp.clip(normal_draw, -4.0, 4.0)


def draw_strip_map(key, part):
    rows = jnp.arange(NY, dtype=jnp.int32)
    block = rows // CY
    inside = rows % CY
    jitter = jax.random.randint(key, (NY,), -1, 2, dtype=jnp.int32)
    value = block * (CY // RATIO) + inside // RATIO + jitter
    return jnp.clip(value, 0, NP - 1).astype(jnp.int32)


def set_ends(array, key, low, largest):
    extent = array.shape
    spot = [jax.random.randint(jax.random.fold_in(key, axis), (), 0, extent[axis]) for axis in range(len(extent))]
    array = array.at[tuple(spot)].set(low)
    longest = extent.index(max(extent))
    spot[longest] = (spot[longest] + 1) % extent[longest]
    return array.at[tuple(spot)].set(largest)


def shard_levels(key, dims, split, smallest, largest):
    def one(position, blocks):
        draws = jax.random.uniform(jax.random.fold_in(jax.random.fold_in(key, 6), position), (blocks,), jnp.float32, smallest / len(split), largest / len(split))
        return jnp.repeat(jnp.exp(draws), dims[position] // blocks).reshape((-1,) + (1,) * (len(dims) - position - 1))

    factor_of = one(*split[0])
    for cut in split[1:]:
        factor_of = factor_of * one(*cut)
    return factor_of


def rank_table(number_of, lean):
    weights = [(1 << 20) // math.isqrt(rank ** lean) + 1 for rank in range(1, number_of + 1)]
    spread = 1 + sum(weights) // (1 << 30)
    return np.cumsum(np.array([max(1, weight // spread) for weight in weights]))


def skewed_ids(key, shape, amount, skew):
    grid = rank_table(amount, skew)
    ticket = jax.random.randint(jax.random.fold_in(key, 1), shape, 0, int(grid[amount - 1]))
    rank = jnp.searchsorted(jnp.asarray(grid, jnp.int32), ticket, side="right")
    return jax.random.permutation(jax.random.fold_in(key, 2), amount)[rank].astype(jnp.int32)


def bell_draw(rng, shape, scale, limit, cuts=(), held_as=jnp.bfloat16):
    level = shard_levels(rng, shape, cuts, -0.22, 0.18) if cuts else 1.0
    values = jax.random.normal(rng, shape, jnp.float32) * scale * level
    return jnp.minimum(jnp.maximum(values, -limit), limit).astype(held_as)


def setup_inputs(seed: int = 0) -> dict:
    streams_of = jax.random.split(jax.random.key(seed), 13)
    sea_level = draw_sea_level(jax.random.fold_in(streams_of[12], 71), 0)
    transport_x = bell_draw(streams_of[1], (NY, NX), 1.0, 5.0, ((0, 96), (1, 8)), jnp.float32)
    transport_y = bell_draw(streams_of[2], (NY, NX), 1.0, 5.0, ((0, 96), (1, 8)), jnp.float32)
    friction = jnp.clip(jnp.exp(math.log(0.5) - 2.3025851 * jax.random.uniform(streams_of[3], (NY, NX), jnp.float32) ** shard_levels(streams_of[3], (NY, NX), ((0, 96), (1, 8)), -0.2, 0.2)), 0.05, 0.5)
    levels = set_ends(jax.random.randint(streams_of[4], (NY, NX), 15, 61), jax.random.fold_in(streams_of[4], 1), 15, 60).astype(jnp.int32)
    strip_map = draw_strip_map(jax.random.fold_in(streams_of[12], 71), 0)
    parent_strip = bell_draw(streams_of[6], (2, SUBSTEPS, 2, NP), 1.0, 5.0, ((3, 768),), jnp.float32)
    plat_tile = set_ends(skewed_ids(streams_of[7], (PLAT,), N_GY * N_GX, 2), jax.random.fold_in(streams_of[7], 3), 0, (N_GY * N_GX) - 1).astype(jnp.int32)
    plat_row = set_ends(jax.random.randint(streams_of[8], (PLAT,), 0, CY), jax.random.fold_in(streams_of[8], 1), 0, CY - 1).astype(jnp.int32)
    plat_col = set_ends(jax.random.randint(streams_of[9], (PLAT,), 0, CX), jax.random.fold_in(streams_of[9], 1), 0, CX - 1).astype(jnp.int32)
    plat_drag = jnp.clip(jnp.exp(math.log(0.5) - 2.3025851 * jax.random.uniform(streams_of[10], (LEVELS, PLAT), jnp.float32) ** shard_levels(streams_of[10], (LEVELS, PLAT), ((1, 768),), -0.2, 0.2)), 0.05, 0.5)
    plat_shear = bell_draw(streams_of[11], (2, LEVELS, PLAT), 0.5, 3.0, ((2, 768),), jnp.float32)
    return dict(sea_level=sea_level, transport_x=transport_x, transport_y=transport_y, friction=friction, levels=levels, strip_map=strip_map, parent_strip=parent_strip, plat_tile=plat_tile, plat_row=plat_row, plat_col=plat_col, plat_drag=plat_drag, plat_shear=plat_shear)


C_MASS = 0.5
C_MOMENTUM = 0.8
FRIC_STEP = 0.5
LOAD_GAIN = 0.5
FLATHER = 0.7

def morison(ubar, vbar, wet_count, drag, shear):
    depth_index = jnp.arange(LEVELS, dtype=jnp.float32)[:, None]
    wet = depth_index < wet_count[None, :]
    ux = ubar[None, :] + shear[0]
    uy = vbar[None, :] + shear[1]
    speed = jnp.sqrt(ux * ux + uy * uy)
    load_x = lax.optimization_barrier(jnp.sum(jnp.where(wet, drag * speed * ux, 0.0), axis=0)) / LEVELS
    load_y = lax.optimization_barrier(jnp.sum(jnp.where(wet, drag * speed * uy, 0.0), axis=0)) / LEVELS
    return jnp.stack([load_x, load_y])

def reference(sea_level, transport_x, transport_y, friction, levels, strip_map, parent_strip, plat_tile, plat_row, plat_col, plat_drag, plat_shear):
    depth = levels.astype(jnp.float32) / LEVELS
    grid_row = (plat_tile // N_GX * CY + plat_row).astype(jnp.int32)
    grid_col = (plat_tile % N_GX * CX + plat_col).astype(jnp.int32)
    plat_depth = depth[grid_row, grid_col]
    ubar = transport_x[grid_row, grid_col] / plat_depth
    vbar = transport_y[grid_row, grid_col] / plat_depth
    wet_count = levels[grid_row, grid_col].astype(jnp.float32)
    loads = morison(ubar, vbar, wet_count, plat_drag, plat_shear)
    force_x = jnp.zeros_like(sea_level).at[grid_row, grid_col].add(loads[0])
    force_y = jnp.zeros_like(sea_level).at[grid_row, grid_col].add(loads[1])
    bound = jnp.take(parent_strip, strip_map, axis=3)
    eta, flow_u, flow_v = (sea_level, transport_x, transport_y)
    for step in range(SUBSTEPS):
        pad_u = jnp.pad(flow_u, 1)
        pad_v = jnp.pad(flow_v, 1)
        mid = eta - C_MASS * (pad_u[1:-1, 2:] - pad_u[1:-1, :-2] + (pad_v[2:, 1:-1] - pad_v[:-2, 1:-1]))
        pad_m = jnp.pad(mid, 1)
        denom = 1.0 + FRIC_STEP * friction * jnp.sqrt(flow_u * flow_u + flow_v * flow_v) / (depth * depth)
        new_u = (flow_u - C_MOMENTUM * depth * (pad_m[1:-1, 2:] - pad_m[1:-1, :-2]) - LOAD_GAIN * force_x) / denom
        new_v = (flow_v - C_MOMENTUM * depth * (pad_m[2:, 1:-1] - pad_m[:-2, 1:-1]) - LOAD_GAIN * force_y) / denom
        west = bound[0, step, 1] - FLATHER * jnp.sqrt(depth[:, 0]) * (mid[:, 0] - bound[0, step, 0])
        east = bound[1, step, 1] + FLATHER * jnp.sqrt(depth[:, -1]) * (mid[:, -1] - bound[1, step, 0])
        new_u = new_u.at[:, 0].set(west).at[:, -1].set(east)
        eta, flow_u, flow_v = (mid, new_u, new_v)
    return (eta, flow_u, flow_v)
```

```python
import functools

import jax
import jax.numpy as jnp
from jax import lax
from jax.experimental import pallas as pl
from jax.experimental.pallas import tpu as pltpu
from jax.sharding import PartitionSpec as P

SUBSTEPS = 4
LEVELS = 60

C_MASS = 0.5
C_MOMENTUM = 0.8
FRIC_STEP = 0.5
LOAD_GAIN = 0.5
FLATHER = 0.7

ROWS = 120
COLS = 256
N_GX = 8
N_GY = 96
HELD = 4
PLAT = N_GY * N_GX * HELD
COL_PLAT = N_GY * HELD

HALO = 2 * SUBSTEPS
EXT = ROWS + 2 * HALO
WIDE = COLS + 128
GROUP = 48
FIELDS = 5
SPAN = FIELDS * HALO
CELL_ROW = GROUP
STRIP_ROW = GROUP + 9
SLOT_ROWS = 64
CHUNK = 512


def iota(shape, dim):
    return lax.broadcasted_iota(jnp.int32, shape, dim)


def three_parts(x):
    high = x.astype(jnp.bfloat16).astype(jnp.float32)
    rest = x - high
    middle = rest.astype(jnp.bfloat16).astype(jnp.float32)
    return [high, middle, rest - middle]


def decode(code):
    col = jnp.bitwise_and(code, COLS - 1)
    row = jnp.bitwise_and(jnp.right_shift(code, 8), 127)
    tile_x = jnp.bitwise_and(jnp.right_shift(code, 15), N_GX - 1)
    tile_y = jnp.right_shift(code, 18)
    return tile_y, tile_x, row, col


def column_of(row_vector):
    return jnp.transpose(jnp.broadcast_to(row_vector, (128, 128)))


def row_halo_kernel(eta, flow_u, flow_v, friction, levels, smap, top, bottom):
    last = ROWS - HALO
    for f, ref in enumerate((eta, flow_u, flow_v, friction, levels)):
        top[f * HALO : (f + 1) * HALO, :] = ref[:HALO, :].astype(jnp.float32)
        bottom[f * HALO : (f + 1) * HALO, :] = ref[last:, :].astype(jnp.float32)
    column = column_of(smap[...].astype(jnp.float32))
    for half in (slice(0, 128), slice(128, 256)):
        top[FIELDS * HALO :, half] = column[:HALO]
        bottom[FIELDS * HALO :, half] = column[last:ROWS]


def extended(f, ref, up, down):
    part = slice(f * HALO, (f + 1) * HALO)
    return jnp.concatenate([up[part, :], ref[...].astype(jnp.float32), down[part, :]], axis=0)


def cell_kernel(pos, eta, flow_u, flow_v, friction, levels, up, down, code, raw, slots):
    gy = pos[0]
    gx = pos[1]
    wide = [
        extended(f, ref, up, down)
        for f, ref in enumerate((eta, flow_u, flow_v, friction, levels))
    ]
    stack = three_parts(wide[1]) + three_parts(wide[2]) + [wide[4]]
    stack.append(jnp.zeros((HALO, COLS), jnp.float32))
    table = jnp.concatenate(stack, axis=0).astype(jnp.bfloat16)
    for start in range(0, PLAT, CHUNK):
        tile_y, tile_x, row, col = decode(code[:, start : start + CHUNK])
        place = (tile_y - gy) * ROWS + row + HALO
        near = (tile_x == gx) & (place >= 0) & (place < EXT)
        hot = iota((COLS, CHUNK), 0) == jnp.where(near, col, -1)
        found = jnp.dot(
            table, hot.astype(jnp.bfloat16), preferred_element_type=jnp.float32
        )
        mine = iota((EXT, CHUNK), 0) == place
        parts = [found[n * EXT : (n + 1) * EXT] for n in range(7)]
        values = [
            parts[0] + parts[1] + parts[2],
            parts[3] + parts[4] + parts[5],
            parts[6],
        ]
        for f, value in enumerate(values):
            line = jnp.sum(jnp.where(mine, value, 0.0), axis=0, keepdims=True)
            for b in range(CHUNK // 128):
                block = start // 128 + b
                r = CELL_ROW + 3 * f + block % 3
                slots[block // 3, r : r + 1, :] = line[:, b * 128 : (b + 1) * 128]
    lane = iota((GROUP, 128), 1)
    west = jnp.zeros((GROUP, 128), jnp.float32)
    east = jnp.zeros((GROUP, 128), jnp.float32)
    for f in range(FIELDS):
        tall = jnp.concatenate(
            [wide[f], jnp.zeros((3 * GROUP - EXT, COLS), jnp.float32)], axis=0
        )
        for g in range(3):
            at = g * SPAN + f * HALO
            rows = slice(g * GROUP, (g + 1) * GROUP)
            mask = (lane >= at) & (lane < at + HALO)
            moved = pltpu.roll(tall[rows, :128], at, 1)
            west = jnp.where(mask, moved, west)
            moved = pltpu.roll(tall[rows, 128:], (at + HALO) % 128, 1)
            east = jnp.where(mask, moved, east)
    for j in range(N_GX):
        slots[j, :GROUP, :] = jnp.where(j > gx, east, west)
    lane = iota((1, 128), 1)
    for b in range(5):
        block = raw[jnp.clip(gy - 2 + b, 0, N_GY - 1)]
        strip = jnp.zeros((1, 128), jnp.float32)
        for t in range(6):
            moved = pltpu.roll(block[t : t + 1, :], (4 * t - 60) % 128, 1)
            strip = jnp.where(jnp.right_shift(jnp.bitwise_and(lane, 63), 2) == t, moved, strip)
        for j in range(N_GX):
            slots[j, STRIP_ROW + b : STRIP_ROW + b + 1, :] = strip
    for j in range(N_GX):
        slots[j, STRIP_ROW + 5 :, :] = jnp.zeros((SLOT_ROWS - STRIP_ROW - 5, 128), jnp.float32)


def load_kernel(raw, cells, slots):
    total = cells[0, CELL_ROW : CELL_ROW + 9, :]
    for j in range(1, N_GX):
        total = total + cells[j, CELL_ROW : CELL_ROW + 9, :]
    lines = []
    for f in range(3):
        line = jnp.concatenate([total[3 * f + q : 3 * f + q + 1, :] for q in range(3)], axis=1)
        for i in range(HELD):
            part = line[:, i * N_GY : (i + 1) * N_GY]
            lines.append(
                jnp.concatenate([part, jnp.zeros((1, 128 - N_GY), jnp.float32)], axis=1)
            )
    lines.append(jnp.zeros((128 - len(lines), 128), jnp.float32))
    columns = jnp.transpose(jnp.concatenate(lines, axis=0))[:N_GY]
    lane = iota((N_GY, 128), 1)
    low = lane < 64
    level = jnp.bitwise_and(lane, 63).astype(jnp.float32)
    result = jnp.zeros((N_GY, 128), jnp.float32)
    for q in range(2):
        u, v, wet = [
            jnp.where(
                low,
                columns[:, f * HELD + 2 * q : f * HELD + 2 * q + 1],
                columns[:, f * HELD + 2 * q + 1 : f * HELD + 2 * q + 2],
            )
            for f in range(3)
        ]
        depth = jnp.maximum(wet, 1.0) / LEVELS
        ux = u / depth + raw[:, 2 + q, :]
        uy = v / depth + raw[:, 4 + q, :]
        drag = jnp.where(level < wet, raw[:, q, :] * jnp.sqrt(ux * ux + uy * uy), 0.0)
        for c, flow in enumerate((ux, uy)):
            product = drag * flow
            for h in range(2):
                share = jnp.where(low, product, 0.0) if h == 0 else jnp.where(low, 0.0, product)
                load = jnp.sum(share, axis=1, keepdims=True) / LEVELS
                result = jnp.where(lane == c * HELD + 2 * q + h, load, result)
    result = jnp.concatenate([result, jnp.zeros((128 - N_GY, 128), jnp.float32)], axis=0)
    rows = jnp.transpose(result)
    out = []
    for c in range(2):
        line = jnp.concatenate(
            [rows[c * HELD + i : c * HELD + i + 1, :N_GY] for i in range(HELD)], axis=1
        )
        out += [line[:, q * 128 : (q + 1) * 128] for q in range(3)]
    out.append(jnp.zeros((2, 128), jnp.float32))
    block = jnp.concatenate(out, axis=0)
    for j in range(N_GX):
        slots[j] = block


def step_kernel(
    pos, eta, flow_u, flow_v, friction, levels, smap, up, down, code, cells, loads,
    out_eta, out_u, out_v, force,
):
    gy = pos[0]
    gx = pos[1]
    for start in range(0, PLAT, CHUNK):
        tile_y, tile_x, row, col = decode(code[:, start : start + CHUNK])
        place = (tile_y - gy) * ROWS + row + HALO
        across = (tile_x - gx) * COLS + col
        near = (across >= -HALO) & (across < COLS + HALO)
        across = jnp.where(near, jnp.where(across < 0, across + WIDE, across), -1)
        mine = iota((EXT, CHUNK), 0) == place
        left = []
        for c in range(2):
            line = jnp.concatenate(
                [
                    loads[b // 3, 3 * c + b % 3 : 3 * c + b % 3 + 1, :]
                    for b in range(start // 128, (start + CHUNK) // 128)
                ],
                axis=1,
            )
            left += [jnp.where(mine, part, 0.0) for part in three_parts(line)]
        left = jnp.concatenate(left, axis=0).astype(jnp.bfloat16)
        right = (iota((WIDE, CHUNK), 0) == across).astype(jnp.bfloat16)
        product = lax.dot_general(
            left, right, (((1,), (1,)), ((), ())), preferred_element_type=jnp.float32
        )
        if start == 0:
            force[...] = product
        else:
            force[...] += product
    part = [force[n * EXT : (n + 1) * EXT, :] for n in range(6)]
    force_x = LOAD_GAIN * (part[0] + part[1] + part[2])
    force_y = LOAD_GAIN * (part[3] + part[4] + part[5])

    from_west = cells[jnp.maximum(gx - 1, 0), :GROUP, :]
    from_east = cells[jnp.minimum(gx + 1, N_GX - 1), :GROUP, :]
    lane = iota((GROUP, 128), 1)

    def widened(f, ref):
        side = []
        for g in range(3):
            at = g * SPAN + f * HALO
            east = pltpu.roll(from_east, (-at) % 128, 1)
            west = pltpu.roll(from_west, (120 - at) % 128, 1)
            side.append(jnp.where(lane < HALO, east, jnp.where(lane >= 120, west, 0.0)))
        side = jnp.concatenate(side, axis=0)[:EXT]
        return jnp.concatenate([extended(f, ref, up, down), side], axis=1)

    e, u, v, fric, lev = [
        widened(f, ref) for f, ref in enumerate((eta, flow_u, flow_v, friction, levels))
    ]
    row = iota((EXT, WIDE), 0)
    lane = iota((EXT, WIDE), 1)
    inside = ((row >= HALO) | (gy > 0)) & ((row < HALO + ROWS) | (gy < N_GY - 1))
    inside = inside & (
        (lane < COLS)
        | ((lane < COLS + HALO) & (gx < N_GX - 1))
        | ((lane >= WIDE - HALO) & (gx > 0))
    )
    e = jnp.where(inside, e, 0.0)
    u = jnp.where(inside, u, 0.0)
    v = jnp.where(inside, v, 0.0)
    depth = jnp.where(inside, lev / LEVELS, 1.0)
    rub = jnp.where(inside, FRIC_STEP * fric / (depth * depth), 1.0)
    push = C_MOMENTUM * depth

    ends = FIELDS * HALO
    ids = jnp.concatenate(
        [up[ends:, :128], column_of(smap[...].astype(jnp.float32))[:ROWS], down[ends:, :128]],
        axis=0,
    ).astype(jnp.int32)
    parents = jnp.concatenate(
        [cells[j, STRIP_ROW : STRIP_ROW + 5, :] for j in range(N_GX)]
        + [jnp.zeros((128 - 5 * N_GX, 128), jnp.float32)],
        axis=0,
    )
    source = iota((EXT, 128), 1)
    bound = jnp.zeros((EXT, 128), jnp.float32)
    slot_lane = jnp.right_shift(jnp.bitwise_and(iota((128, 128), 1), 63), 3)
    for j in range(3):
        column = jnp.zeros((EXT, 128), jnp.int32)
        for step in range(1, N_GX):
            column = column + (source >= 5 * step).astype(jnp.int32)
        block = gy - 2 + source - 5 * column
        held = (ids == (block * N_GX + column) * 3 + j) & (source < 5 * N_GX)
        part = jnp.where(slot_lane == j, parents, 0.0)
        bound = bound + sum(
            jnp.dot(
                held.astype(jnp.bfloat16),
                piece.astype(jnp.bfloat16),
                preferred_element_type=jnp.float32,
            )
            for piece in three_parts(part)
        )
    bound = bound + pltpu.roll(bound, 120, 1) + pltpu.roll(bound, 112, 1)

    side_lane = iota((EXT, 128), 1)
    at_west = (side_lane == 0) & (gx == 0)
    at_east = (side_lane == 127) & (gx == N_GX - 1)
    radiate_west = FLATHER * jnp.sqrt(depth[:, :128])
    radiate_east = FLATHER * jnp.sqrt(depth[:, 128:COLS])
    for step in range(SUBSTEPS):
        spread = pltpu.roll(u, WIDE - 1, 1) - pltpu.roll(u, 1, 1)
        spread = spread + (pltpu.roll(v, EXT - 1, 0) - pltpu.roll(v, 1, 0))
        mid = jnp.where(inside, e - C_MASS * spread, 0.0)
        denom = 1.0 + rub * jnp.sqrt(u * u + v * v)
        slope_x = pltpu.roll(mid, WIDE - 1, 1) - pltpu.roll(mid, 1, 1)
        slope_y = pltpu.roll(mid, EXT - 1, 0) - pltpu.roll(mid, 1, 0)
        scale = 1.0 / denom
        new_u = (u - push * slope_x - force_x) * scale
        new_v = (v - push * slope_y - force_y) * scale
        west = bound[:, 2 * step + 1 : 2 * step + 2] - radiate_west * (
            mid[:, :128] - bound[:, 2 * step : 2 * step + 1]
        )
        east = bound[:, 64 + 2 * step + 1 : 64 + 2 * step + 2] + radiate_east * (
            mid[:, 128:COLS] - bound[:, 64 + 2 * step : 64 + 2 * step + 1]
        )
        new_u = jnp.concatenate(
            [
                jnp.where(at_west, west, new_u[:, :128]),
                jnp.where(at_east, east, new_u[:, 128:COLS]),
                new_u[:, COLS:],
            ],
            axis=1,
        )
        e = mid
        u = jnp.where(inside, new_u, 0.0)
        v = jnp.where(inside, new_v, 0.0)
    out_eta[...] = e[HALO : HALO + ROWS, :COLS]
    out_u[...] = u[HALO : HALO + ROWS, :COLS]
    out_v[...] = v[HALO : HALO + ROWS, :COLS]


def call(kernel, out_shape, smem, count, name, scratch=()):
    vmem = pl.BlockSpec(memory_space=pltpu.VMEM)
    specs = [pl.BlockSpec(memory_space=pltpu.SMEM)] * smem + [vmem] * (count - smem)
    many = isinstance(out_shape, list)
    return pl.pallas_call(
        kernel,
        out_shape=out_shape,
        in_specs=specs,
        out_specs=[vmem] * len(out_shape) if many else vmem,
        scratch_shapes=list(scratch),
        compiler_params=pltpu.CompilerParams(vmem_limit_bytes=32 * 1024 * 1024),
        name=name,
    )


def f32(*shape):
    return jax.ShapeDtypeStruct(shape, jnp.float32)


def on_device(
    sea_level,
    transport_x,
    transport_y,
    friction,
    levels,
    strip_map,
    parent_strip,
    plat_tile,
    plat_row,
    plat_col,
    plat_drag,
    plat_shear,
):
    pos = jnp.stack([lax.axis_index("gy"), lax.axis_index("gx")]).astype(jnp.int32)
    fields = (sea_level, transport_x, transport_y, friction, levels)
    smap = jnp.pad(strip_map, (0, 128 - ROWS)).reshape(1, 128)
    top, bottom = call(row_halo_kernel, [f32(48, COLS), f32(48, COLS)], 0, 6, "row_halo")(
        *fields, smap
    )
    count = lax.axis_size("gy")
    upward = [(i, i + 1) for i in range(count - 1)]
    downward = [(target, source) for source, target in upward]
    up = lax.ppermute(bottom, "gy", upward)
    down = lax.ppermute(top, "gy", downward)

    held = jnp.concatenate([plat_drag[None], plat_shear], axis=0)
    held = held.transpose(0, 2, 1).reshape(6, 2, LEVELS)
    strip = parent_strip.reshape(2, 2, 4, 3).transpose(3, 1, 0, 2).reshape(6, 2, 4)
    held = jnp.concatenate([held, strip], axis=2).reshape(1, 6, 128)
    raw = lax.all_to_all(jnp.broadcast_to(held, (N_GY, 6, 128)), "gy", 0, 0, tiled=True)

    code = (plat_tile << 15) | (plat_row << 8) | plat_col
    code = code.reshape(N_GY, N_GX, HELD).transpose(1, 2, 0).reshape(1, PLAT)
    slots = call(cell_kernel, f32(N_GX, SLOT_ROWS, 128), 1, 10, "cells")(
        pos, *fields, up, down, code, raw
    )
    cells = lax.all_to_all(slots, "gx", 0, 0, tiled=True)
    slots = call(load_kernel, f32(N_GX, 8, 128), 0, 2, "loads")(raw, cells)
    loads = lax.all_to_all(slots, "gx", 0, 0, tiled=True)
    out = f32(ROWS, COLS)
    return tuple(
        call(
            step_kernel,
            [out, out, out],
            1,
            12,
            "steps",
            [pltpu.VMEM((6 * EXT, WIDE), jnp.float32)],
        )(pos, *fields, smap, up, down, code, cells, loads)
    )


def solution(mesh):
    return jax.shard_map(
        on_device,
        mesh=mesh,
        in_specs=(
            P("gy", "gx"),
            P("gy", "gx"),
            P("gy", "gx"),
            P("gy", "gx"),
            P("gy", "gx"),
            P("gy"),
            P(None, None, None, ("gy", "gx")),
            P(),
            P(),
            P(),
            P(None, ("gy", "gx")),
            P(None, None, ("gy", "gx")),
        ),
        out_specs=(P("gy", "gx"), P("gy", "gx"), P("gy", "gx")),
        check_vma=False,
    )
```

```python
import functools

import jax
import jax.numpy as jnp
from jax import lax
from jax.experimental import pallas as pl
from jax.experimental.pallas import tpu as pltpu
from jax.sharding import PartitionSpec as P

SUBSTEPS = 4
LEVELS = 60

C_MASS = 0.5
C_MOMENTUM = 0.8
FRIC_STEP = 0.5
LOAD_GAIN = 0.5
FLATHER = 0.7

ROWS = 120
COLS = 256
N_GX = 8
N_GY = 96
HELD = 4
PLAT = N_GY * N_GX * HELD
COL_PLAT = N_GY * HELD

HALO = 2 * SUBSTEPS
EXT = ROWS + 2 * HALO
WIDE = COLS + 128
GROUP = 48
FIELDS = 5
SPAN = FIELDS * HALO
CELL_ROW = GROUP
STRIP_ROW = GROUP + 16
SLOT_ROWS = 72
BACK_ROWS = 8
CHUNK = 512


def iota(shape, dim):
    return lax.broadcasted_iota(jnp.int32, shape, dim)


def three_parts(x):
    high = x.astype(jnp.bfloat16).astype(jnp.float32)
    rest = x - high
    middle = rest.astype(jnp.bfloat16).astype(jnp.float32)
    return [high, middle, rest - middle]


def decode(code):
    col = jnp.bitwise_and(code, COLS - 1)
    row = jnp.bitwise_and(jnp.right_shift(code, 8), 127)
    tile_x = jnp.bitwise_and(jnp.right_shift(code, 15), N_GX - 1)
    tile_y = jnp.right_shift(code, 18)
    return tile_y, tile_x, row, col


def column_of(row_vector):
    row_vector = jnp.concatenate([row_vector, jnp.zeros((1, 128 - ROWS), jnp.float32)], axis=1)
    return jnp.transpose(jnp.broadcast_to(row_vector, (128, 128)))


def fetch(pairs, sems):
    copies = [pltpu.make_async_copy(src, dst, sems.at[n]) for n, (src, dst) in enumerate(pairs)]
    for copy in copies:
        copy.start()
    return copies


def raw_kernel(drag_in, shear_in, strip_in, slots, drag, shear, strip, sems):
    pairs = ((drag_in, drag), (shear_in, shear), (strip_in, strip))
    for copy in fetch(pairs, sems):
        copy.wait()
    held = (drag[...], shear[0], shear[1])
    lines = []
    for t in range(6):
        pieces = []
        for h in range(2):
            i = 2 * (t % 2) + h
            pieces.append(held[t // 2][i : i + 1, :])
            pieces.append(strip[h, t // 2][t % 2 : t % 2 + 1, :])
        lines.append(jnp.concatenate(pieces, axis=1))
    block = jnp.concatenate(lines, axis=0)
    for j in range(N_GY):
        slots[j] = block


def row_halo_kernel(
    eta, flow_u, flow_v, friction, levels, smap, top, bottom, low, high, sems
):
    last = ROWS - HALO
    pairs = [(levels.at[pl.ds(0, HALO), :], low), (levels.at[pl.ds(last, HALO), :], high)]
    for f, ref in enumerate((eta, flow_u, flow_v, friction)):
        part = pl.ds(f * HALO, HALO)
        pairs.append((ref.at[pl.ds(0, HALO), :], top.at[part, :]))
        pairs.append((ref.at[pl.ds(last, HALO), :], bottom.at[part, :]))
    copies = fetch(pairs, sems)
    column = column_of(smap[...].astype(jnp.float32))
    for half in (slice(0, 128), slice(128, 256)):
        top[FIELDS * HALO :, half] = column[:HALO]
        bottom[FIELDS * HALO :, half] = column[last:ROWS]
    for copy in copies:
        copy.wait()
    top[4 * HALO : 5 * HALO, :] = low[...].astype(jnp.float32)
    bottom[4 * HALO : 5 * HALO, :] = high[...].astype(jnp.float32)


def extended(f, ref, up, down):
    part = slice(f * HALO, (f + 1) * HALO)
    return jnp.concatenate([up[part, :], ref[...].astype(jnp.float32), down[part, :]], axis=0)


def cell_kernel(pos, code, *refs):
    *fields, up, down, slots = refs
    gy = pos[0]
    gx = pos[1]
    wide = [extended(f, ref, up, down) for f, ref in enumerate(fields)]
    stack = three_parts(wide[1]) + three_parts(wide[2]) + [wide[4]]
    stack.append(jnp.zeros((HALO, COLS), jnp.float32))
    table = jnp.concatenate(stack, axis=0).astype(jnp.bfloat16)
    for start in range(0, PLAT, CHUNK):
        tile_y, tile_x, row, col = decode(code[:, start : start + CHUNK])
        place = (tile_y - gy) * ROWS + row + HALO
        near = (tile_x == gx) & (place >= 0) & (place < EXT)
        hot = iota((COLS, CHUNK), 0) == jnp.where(near, col, -1)
        found = jnp.dot(
            table, hot.astype(jnp.bfloat16), preferred_element_type=jnp.float32
        )
        mine = iota((EXT, CHUNK), 0) == place
        parts = [found[n * EXT : (n + 1) * EXT] for n in range(7)]
        values = [
            parts[0] + parts[1] + parts[2],
            parts[3] + parts[4] + parts[5],
            parts[6],
        ]
        for f, value in enumerate(values):
            line = jnp.sum(jnp.where(mine, value, 0.0), axis=0, keepdims=True)
            for b in range(CHUNK // 128):
                block = start // 128 + b
                r = CELL_ROW + 3 * f + block % 3
                slots[block // 3, r : r + 1, :] = line[:, b * 128 : (b + 1) * 128]
    lane = iota((GROUP, 128), 1)
    west = jnp.zeros((GROUP, 128), jnp.float32)
    east = jnp.zeros((GROUP, 128), jnp.float32)
    for f in range(FIELDS):
        tall = jnp.concatenate(
            [wide[f], jnp.zeros((3 * GROUP - EXT, COLS), jnp.float32)], axis=0
        )
        for g in range(3):
            at = g * SPAN + f * HALO
            rows = slice(g * GROUP, (g + 1) * GROUP)
            mask = (lane >= at) & (lane < at + HALO)
            moved = pltpu.roll(tall[rows, :128], at, 1)
            west = jnp.where(mask, moved, west)
            moved = pltpu.roll(tall[rows, 128:], (at + HALO) % 128, 1)
            east = jnp.where(mask, moved, east)
    for j in range(N_GX):
        slots[j, :GROUP, :] = jnp.where(j > gx, east, west)
    for j in range(N_GX):
        slots[j, CELL_ROW + 9 :, :] = jnp.zeros((SLOT_ROWS - CELL_ROW - 9, 128), jnp.float32)


def strip_kernel(pos, raw, slots_in, slots):
    gy = pos[0]
    blocks = [raw[jnp.clip(gy - 2 + b, 0, N_GY - 1)] for b in range(5)]
    lane = iota((8, 128), 1)
    group = jnp.right_shift(jnp.bitwise_and(lane, 63), 2)
    strip = jnp.zeros((8, 128), jnp.float32)
    for t in range(6):
        lines = [block[t : t + 1, :] for block in blocks] + [jnp.zeros((3, 128), jnp.float32)]
        moved = pltpu.roll(jnp.concatenate(lines, axis=0), (4 * t - LEVELS) % 128, 1)
        strip = jnp.where(group == t, moved, strip)
    for j in range(N_GX):
        slots[j, STRIP_ROW : STRIP_ROW + 8, :] = strip


def load_kernel(cells, raw, slots):
    total = cells[0, CELL_ROW : CELL_ROW + 16, :]
    for j in range(1, N_GX):
        total = total + cells[j, CELL_ROW : CELL_ROW + 16, :]
    lines = []
    for f in range(3):
        line = jnp.concatenate([total[3 * f + q : 3 * f + q + 1, :] for q in range(3)], axis=1)
        for i in range(HELD):
            part = line[:, i * N_GY : (i + 1) * N_GY]
            lines.append(
                jnp.concatenate([part, jnp.zeros((1, 128 - N_GY), jnp.float32)], axis=1)
            )
    lines.append(jnp.zeros((128 - len(lines), 128), jnp.float32))
    columns = jnp.transpose(jnp.concatenate(lines, axis=0))[:N_GY]
    lane = iota((N_GY, 128), 1)
    low = lane < 64
    level = jnp.bitwise_and(lane, 63).astype(jnp.float32)
    result = jnp.zeros((N_GY, 128), jnp.float32)
    for q in range(2):
        u, v, wet = [
            jnp.where(
                low,
                columns[:, f * HELD + 2 * q : f * HELD + 2 * q + 1],
                columns[:, f * HELD + 2 * q + 1 : f * HELD + 2 * q + 2],
            )
            for f in range(3)
        ]
        depth = jnp.maximum(wet, 1.0) / LEVELS
        ux = u / depth + raw[:, 2 + q, :]
        uy = v / depth + raw[:, 4 + q, :]
        drag = jnp.where(level < wet, raw[:, q, :] * jnp.sqrt(ux * ux + uy * uy), 0.0)
        for c, flow in enumerate((ux, uy)):
            product = drag * flow
            for h in range(2):
                share = jnp.where(low, product, 0.0) if h == 0 else jnp.where(low, 0.0, product)
                load = jnp.sum(share, axis=1, keepdims=True) / LEVELS
                result = jnp.where(lane == c * HELD + 2 * q + h, load, result)
    result = jnp.concatenate([result, jnp.zeros((128 - N_GY, 128), jnp.float32)], axis=0)
    rows = jnp.transpose(result)
    out = []
    for c in range(2):
        line = jnp.concatenate(
            [rows[c * HELD + i : c * HELD + i + 1, :N_GY] for i in range(HELD)], axis=1
        )
        out += [line[:, q * 128 : (q + 1) * 128] for q in range(3)]
    out.append(jnp.zeros((2, 128), jnp.float32))
    block = jnp.concatenate(out, axis=0)
    for j in range(N_GX):
        slots[j] = block


def inside_of(gy, gx):
    row = iota((EXT, WIDE), 0)
    lane = iota((EXT, WIDE), 1)
    inside = ((row >= HALO) | (gy > 0)) & ((row < HALO + ROWS) | (gy < N_GY - 1))
    return inside & (
        (lane < COLS)
        | ((lane < COLS + HALO) & (gx < N_GX - 1))
        | ((lane >= WIDE - HALO) & (gx > 0))
    )


def half_step(e, u, v, rub, push, inside):
    spread = pltpu.roll(u, WIDE - 1, 1) - pltpu.roll(u, 1, 1)
    spread = spread + (pltpu.roll(v, EXT - 1, 0) - pltpu.roll(v, 1, 0))
    mid = jnp.where(inside, e - C_MASS * spread, 0.0)
    scale = 1.0 / (1.0 + rub * jnp.sqrt(u * u + v * v))
    slope_x = pltpu.roll(mid, WIDE - 1, 1) - pltpu.roll(mid, 1, 1)
    slope_y = pltpu.roll(mid, EXT - 1, 0) - pltpu.roll(mid, 1, 0)
    return mid, (u - push * slope_x) * scale, (v - push * slope_y) * scale, scale


def ready_kernel(pos, smap, cells, *refs):
    *fields, up, down, out = refs
    gy = pos[0]
    gx = pos[1]
    from_west = cells[jnp.maximum(gx - 1, 0), :GROUP, :]
    from_east = cells[jnp.minimum(gx + 1, N_GX - 1), :GROUP, :]
    lane = iota((GROUP, 128), 1)

    def widened(f, ref):
        side = []
        for g in range(3):
            at = g * SPAN + f * HALO
            east = pltpu.roll(from_east, (-at) % 128, 1)
            west = pltpu.roll(from_west, (120 - at) % 128, 1)
            side.append(jnp.where(lane < HALO, east, jnp.where(lane >= 120, west, 0.0)))
        side = jnp.concatenate(side, axis=0)[:EXT]
        return jnp.concatenate([extended(f, ref, up, down), side], axis=1)

    e, u, v, fric, lev = [widened(f, ref) for f, ref in enumerate(fields)]
    inside = inside_of(gy, gx)
    e = jnp.where(inside, e, 0.0)
    u = jnp.where(inside, u, 0.0)
    v = jnp.where(inside, v, 0.0)
    depth = jnp.where(inside, lev / LEVELS, 1.0)
    rub = jnp.where(inside, FRIC_STEP * fric / (depth * depth), 1.0)
    push = C_MOMENTUM * depth
    mid, u, v, scale = half_step(e, u, v, rub, push, inside)
    for n, field in enumerate((mid, u, v, scale, rub, push)):
        out[n] = field

    ends = FIELDS * HALO
    ids = jnp.concatenate(
        [up[ends:, :128], column_of(smap[...].astype(jnp.float32))[:ROWS], down[ends:, :128]],
        axis=0,
    ).astype(jnp.int32)
    parents = jnp.concatenate(
        [cells[j, STRIP_ROW : STRIP_ROW + 5, :] for j in range(N_GX)]
        + [jnp.zeros((128 - 5 * N_GX, 128), jnp.float32)],
        axis=0,
    )
    source = iota((EXT, 128), 1)
    column = jnp.zeros((EXT, 128), jnp.int32)
    for step in range(1, N_GX):
        column = column + (source >= 5 * step).astype(jnp.int32)
    first = ((gy - 2 + source - 5 * column) * N_GX + column) * 3
    slot_lane = jnp.right_shift(jnp.bitwise_and(iota((128, 128), 1), 63), 3)
    bound = jnp.zeros((EXT, 128), jnp.float32)
    for j in range(3):
        held = (ids == first + j) & (source < 5 * N_GX)
        for piece in three_parts(jnp.where(slot_lane == j, parents, 0.0)):
            bound = bound + jnp.dot(
                held.astype(jnp.bfloat16),
                piece.astype(jnp.bfloat16),
                preferred_element_type=jnp.float32,
            )
    bound = bound + pltpu.roll(bound, 120, 1) + pltpu.roll(bound, 112, 1)

    out[6, :, :128] = bound


def step_kernel(pos, code, loads, ready, out_eta, out_u, out_v, force):
    gy = pos[0]
    gx = pos[1]
    for start in range(0, PLAT, CHUNK):
        tile_y, tile_x, row, col = decode(code[:, start : start + CHUNK])
        place = (tile_y - gy) * ROWS + row + HALO
        across = (tile_x - gx) * COLS + col
        near = (across >= -HALO) & (across < COLS + HALO)
        across = jnp.where(near, jnp.where(across < 0, across + WIDE, across), -1)
        right = (iota((WIDE, CHUNK), 0) == across).astype(jnp.bfloat16)
        mine = iota((EXT, CHUNK), 0) == place
        left = []
        for c in range(2):
            line = jnp.concatenate(
                [
                    loads[b // 3, 3 * c + b % 3 : 3 * c + b % 3 + 1, :]
                    for b in range(start // 128, (start + CHUNK) // 128)
                ],
                axis=1,
            )
            left += [jnp.where(mine, part, 0.0) for part in three_parts(line)]
        left = jnp.concatenate(left, axis=0).astype(jnp.bfloat16)
        product = lax.dot_general(
            left,
            right,
            (((1,), (1,)), ((), ())),
            preferred_element_type=jnp.float32,
        )
        if start == 0:
            force[...] = product
        else:
            force[...] += product
    part = [force[n * EXT : (n + 1) * EXT, :] for n in range(6)]
    force_x = LOAD_GAIN * (part[0] + part[1] + part[2])
    force_y = LOAD_GAIN * (part[3] + part[4] + part[5])

    mid, flow_u, flow_v, scale, rub, push = [ready[n] for n in range(6)]
    bound = ready[6, :, :128]
    inside = inside_of(gy, gx)
    side_lane = iota((EXT, 128), 1)
    at_west = (side_lane == 0) & (gx == 0)
    at_east = (side_lane == 127) & (gx == N_GX - 1)
    root = FLATHER * jnp.sqrt(push[:, :COLS] * (1.0 / C_MOMENTUM))

    def finish(step, mid, u, v):
        sea, flow = [bound[:, 4 * f + step : 4 * f + step + 1] for f in range(2)]
        west = flow - root[:, :128] * (mid[:, :128] - sea)
        sea, flow = [bound[:, 64 + 4 * f + step : 64 + 4 * f + step + 1] for f in range(2)]
        east = flow + root[:, 128:] * (mid[:, 128:COLS] - sea)
        u = jnp.concatenate(
            [
                jnp.where(at_west, west, u[:, :128]),
                jnp.where(at_east, east, u[:, 128:COLS]),
                u[:, COLS:],
            ],
            axis=1,
        )
        return jnp.where(inside, u, 0.0), jnp.where(inside, v, 0.0)

    e = mid
    u, v = finish(0, e, flow_u - force_x * scale, flow_v - force_y * scale)
    for step in range(1, SUBSTEPS):
        e, u, v, s = half_step(e, u, v, rub, push, inside)
        u, v = finish(step, e, u - force_x * s, v - force_y * s)
    out_eta[...] = e[HALO : HALO + ROWS, :COLS]
    out_u[...] = u[HALO : HALO + ROWS, :COLS]
    out_v[...] = v[HALO : HALO + ROWS, :COLS]


def call(kernel, out_shape, spaces, name, scratch=(), limit=12, cycles=1, **kw):
    many = isinstance(out_shape, list)
    out_spec = pl.BlockSpec(memory_space=pltpu.VMEM)
    return pl.pallas_call(
        kernel,
        out_shape=out_shape,
        in_specs=[pl.BlockSpec(memory_space=space) for space in spaces],
        out_specs=[out_spec] * len(out_shape) if many else out_spec,
        scratch_shapes=list(scratch),
        compiler_params=pltpu.CompilerParams(vmem_limit_bytes=limit * 1024 * 1024),
        cost_estimate=pl.CostEstimate(
            flops=cycles * 10**8, bytes_accessed=cycles * 2 * 10**6, transcendentals=0
        ),
        name=name,
        **kw,
    )


def f32(*shape):
    return jax.ShapeDtypeStruct(shape, jnp.float32)


def on_device(
    sea_level,
    transport_x,
    transport_y,
    friction,
    levels,
    strip_map,
    parent_strip,
    plat_tile,
    plat_row,
    plat_col,
    plat_drag,
    plat_shear,
):
    pos = jnp.stack([lax.axis_index("gy"), lax.axis_index("gx")]).astype(jnp.int32)
    fields = (sea_level, transport_x, transport_y, friction, levels)
    smap = strip_map.reshape(1, ROWS)
    scalar, vmem, hbm = pltpu.SMEM, pltpu.VMEM, pltpu.HBM
    sems = pltpu.SemaphoreType.DMA

    held = call(
        raw_kernel,
        f32(N_GY, 6, 128),
        [hbm] * 3,
        "raw",
        [
            pltpu.VMEM((HELD, LEVELS), jnp.float32),
            pltpu.VMEM((2, HELD, LEVELS), jnp.float32),
            pltpu.VMEM((2, 3, 2, SUBSTEPS), jnp.float32),
            sems((3,)),
        ],
        60,
    )(plat_drag.T, plat_shear.transpose(0, 2, 1), parent_strip.transpose(0, 3, 2, 1))
    raw = lax.all_to_all(held, "gy", 0, 0, tiled=True)

    edge = pltpu.VMEM((HALO, COLS), jnp.int32)
    top, bottom = call(
        row_halo_kernel,
        [f32(GROUP, COLS), f32(GROUP, COLS)],
        [hbm] * 5 + [vmem],
        "row_halo",
        [edge, edge, sems((10,))],
        60,
    )(*fields, smap)
    count = lax.axis_size("gy")
    upward = [(i, i + 1) for i in range(count - 1)]
    downward = [(target, source) for source, target in upward]
    near = (*fields, lax.ppermute(bottom, "gy", upward), lax.ppermute(top, "gy", downward))

    code = (plat_tile << 15) | (plat_row << 8) | plat_col
    code = code.reshape(N_GY, N_GX, HELD).transpose(1, 2, 0).reshape(1, PLAT)
    slots = call(
        cell_kernel,
        f32(N_GX, SLOT_ROWS, 128),
        [scalar] + [vmem] * 8,
        "cells",
        cycles=4,
    )(pos, code, *near)
    slots = call(
        strip_kernel,
        f32(N_GX, SLOT_ROWS, 128),
        [scalar, vmem, vmem],
        "strips",
        input_output_aliases={2: 0},
    )(pos, raw, slots)
    cells = lax.all_to_all(slots, "gx", 0, 0, tiled=True)
    slots = call(load_kernel, f32(N_GX, BACK_ROWS, 128), [vmem, vmem], "loads")(cells, raw)
    loads = lax.all_to_all(slots, "gx", 0, 0, tiled=True)
    ready = call(ready_kernel, f32(7, EXT, WIDE), [scalar] + [vmem] * 9, "ready", cycles=4)(
        pos, smap, cells, *near
    )
    out = f32(ROWS, COLS)
    force = pltpu.VMEM((6 * EXT, WIDE), jnp.float32)
    return tuple(
        call(step_kernel, [out, out, out], [scalar] + [vmem] * 3, "steps", [force])(
            pos, code, loads, ready
        )
    )


def solution(mesh):
    return jax.shard_map(
        on_device,
        mesh=mesh,
        in_specs=(
            P("gy", "gx"),
            P("gy", "gx"),
            P("gy", "gx"),
            P("gy", "gx"),
            P("gy", "gx"),
            P("gy"),
            P(None, None, None, ("gy", "gx")),
            P(),
            P(),
            P(),
            P(None, ("gy", "gx")),
            P(None, None, ("gy", "gx")),
        ),
        out_specs=(P("gy", "gx"), P("gy", "gx"), P("gy", "gx")),
        check_vma=False,
    )
```

```python
import functools

import jax
import jax.numpy as jnp
from jax import lax
from jax.experimental import pallas as pl
from jax.experimental.pallas import tpu as pltpu
from jax.sharding import PartitionSpec as P

SUBSTEPS = 4
LEVELS = 60

C_MASS = 0.5
C_MOMENTUM = 0.8
FRIC_STEP = 0.5
LOAD_GAIN = 0.5
FLATHER = 0.7

ROWS = 120
COLS = 256
N_GX = 8
N_GY = 96
HELD = 4
PLAT = N_GY * N_GX * HELD
COL_PLAT = N_GY * HELD

HALO = 2 * SUBSTEPS
EXT = ROWS + 2 * HALO
WIDE = COLS + 128
GROUP = 48
FIELDS = 5
SPAN = FIELDS * HALO
CELL_ROW = GROUP
STRIP_ROW = GROUP + 9
SLOT_ROWS = 64
BACK_ROWS = 8
CHUNK = 512
PARTS = 3


def iota(shape, dim):
    return lax.broadcasted_iota(jnp.int32, shape, dim)


def three_parts(x):
    high = x.astype(jnp.bfloat16).astype(jnp.float32)
    rest = x - high
    middle = rest.astype(jnp.bfloat16).astype(jnp.float32)
    return [high, middle, rest - middle]


def decode(code):
    col = jnp.bitwise_and(code, COLS - 1)
    row = jnp.bitwise_and(jnp.right_shift(code, 8), 127)
    tile_x = jnp.bitwise_and(jnp.right_shift(code, 15), N_GX - 1)
    tile_y = jnp.right_shift(code, 18)
    return tile_y, tile_x, row, col


def column_of(row_vector):
    row_vector = jnp.concatenate([row_vector, jnp.zeros((1, 128 - ROWS), jnp.float32)], axis=1)
    return jnp.transpose(jnp.broadcast_to(row_vector, (128, 128)))


def fetch(pairs, sems):
    copies = [pltpu.make_async_copy(src, dst, sems.at[n]) for n, (src, dst) in enumerate(pairs)]
    for copy in copies:
        copy.start()
    return copies


def raw_kernel(drag_in, shear_in, strip_in, slots, drag, shear, strip, sems):
    pairs = ((drag_in, drag), (shear_in, shear), (strip_in, strip))
    for copy in fetch(pairs, sems):
        copy.wait()
    held = (drag[...], shear[0], shear[1])
    lines = []
    for t in range(6):
        pieces = []
        for h in range(2):
            i = 2 * (t % 2) + h
            pieces.append(held[t // 2][i : i + 1, :])
            pieces.append(strip[h, t // 2][t % 2 : t % 2 + 1, :])
        lines.append(jnp.concatenate(pieces, axis=1))
    block = jnp.concatenate(lines, axis=0)
    for j in range(N_GY):
        slots[j] = block


def row_halo_kernel(eta, flow_u, flow_v, friction, levels, smap, top, bottom):
    last = ROWS - HALO
    for f, ref in enumerate((eta, flow_u, flow_v, friction, levels)):
        part = slice(f * HALO, (f + 1) * HALO)
        top[part, :] = ref[:HALO, :].astype(jnp.float32)
        bottom[part, :] = ref[last:, :].astype(jnp.float32)
    column = column_of(smap[...].astype(jnp.float32))
    for half in (slice(0, 128), slice(128, 256)):
        top[FIELDS * HALO :, half] = column[:HALO]
        bottom[FIELDS * HALO :, half] = column[last:ROWS]


def extended(f, ref, up, down):
    part = slice(f * HALO, (f + 1) * HALO)
    return jnp.concatenate([up[part, :], ref[...].astype(jnp.float32), down[part, :]], axis=0)


def cell_kernel(code, *refs):
    *fields, up, down, slots = refs
    gy = lax.axis_index("gy")
    gx = lax.axis_index("gx")
    wide = [extended(f, ref, up, down) for f, ref in enumerate(fields)]
    stack = three_parts(wide[1]) + three_parts(wide[2]) + [wide[4]]
    stack.append(jnp.zeros((HALO, COLS), jnp.float32))
    table = jnp.concatenate(stack, axis=0).astype(jnp.bfloat16)
    for start in range(0, PLAT, CHUNK):
        tile_y, tile_x, row, col = decode(code[:, start : start + CHUNK])
        place = (tile_y - gy) * ROWS + row + HALO
        near = (tile_x == gx) & (place >= 0) & (place < EXT)
        hot = iota((COLS, CHUNK), 0) == jnp.where(near, col, -1)
        found = jnp.dot(
            table, hot.astype(jnp.bfloat16), preferred_element_type=jnp.float32
        )
        mine = iota((EXT, CHUNK), 0) == place
        parts = [found[n * EXT : (n + 1) * EXT] for n in range(7)]
        values = [
            parts[0] + parts[1] + parts[2],
            parts[3] + parts[4] + parts[5],
            parts[6],
        ]
        for f, value in enumerate(values):
            line = jnp.sum(jnp.where(mine, value, 0.0), axis=0, keepdims=True)
            for b in range(CHUNK // 128):
                block = start // 128 + b
                r = CELL_ROW + 3 * f + block % 3
                slots[block // 3, r : r + 1, :] = line[:, b * 128 : (b + 1) * 128]
    lane = iota((GROUP, 128), 1)
    west = jnp.zeros((GROUP, 128), jnp.float32)
    east = jnp.zeros((GROUP, 128), jnp.float32)
    for f in range(FIELDS):
        tall = jnp.concatenate(
            [wide[f], jnp.zeros((3 * GROUP - EXT, COLS), jnp.float32)], axis=0
        )
        for g in range(3):
            at = g * SPAN + f * HALO
            rows = slice(g * GROUP, (g + 1) * GROUP)
            mask = (lane >= at) & (lane < at + HALO)
            moved = pltpu.roll(tall[rows, :128], at, 1)
            west = jnp.where(mask, moved, west)
            moved = pltpu.roll(tall[rows, 128:], (at + HALO) % 128, 1)
            east = jnp.where(mask, moved, east)
    for j in range(N_GX):
        slots[j, :GROUP, :] = jnp.where(j > gx, east, west)
    for j in range(N_GX):
        slots[j, CELL_ROW + 9 :, :] = jnp.zeros((SLOT_ROWS - CELL_ROW - 9, 128), jnp.float32)


def strip_kernel(raw, slots_in, slots):
    gy = lax.axis_index("gy")
    blocks = [raw[jnp.clip(gy - 2 + b, 0, N_GY - 1)] for b in range(5)]
    lane = iota((8, 128), 1)
    group = jnp.right_shift(jnp.bitwise_and(lane, 63), 2)
    strip = jnp.zeros((8, 128), jnp.float32)
    for t in range(6):
        lines = [block[t : t + 1, :] for block in blocks] + [jnp.zeros((3, 128), jnp.float32)]
        moved = pltpu.roll(jnp.concatenate(lines, axis=0), (4 * t - LEVELS) % 128, 1)
        strip = jnp.where(group == t, moved, strip)
    for j in range(N_GX):
        slots[j, STRIP_ROW : STRIP_ROW + 5, :] = strip[:5]


def load_kernel(cells, raw, slots):
    total = cells[0, CELL_ROW : CELL_ROW + 9, :]
    for j in range(1, N_GX):
        total = total + cells[j, CELL_ROW : CELL_ROW + 9, :]
    lines = []
    for f in range(3):
        line = jnp.concatenate([total[3 * f + q : 3 * f + q + 1, :] for q in range(3)], axis=1)
        for i in range(HELD):
            part = line[:, i * N_GY : (i + 1) * N_GY]
            lines.append(
                jnp.concatenate([part, jnp.zeros((1, 128 - N_GY), jnp.float32)], axis=1)
            )
    lines.append(jnp.zeros((128 - len(lines), 128), jnp.float32))
    columns = jnp.transpose(jnp.concatenate(lines, axis=0))[:N_GY]
    lane = iota((N_GY, 128), 1)
    low = lane < 64
    level = jnp.bitwise_and(lane, 63).astype(jnp.float32)
    result = jnp.zeros((N_GY, 128), jnp.float32)
    for q in range(2):
        u, v, wet = [
            jnp.where(
                low,
                columns[:, f * HELD + 2 * q : f * HELD + 2 * q + 1],
                columns[:, f * HELD + 2 * q + 1 : f * HELD + 2 * q + 2],
            )
            for f in range(3)
        ]
        depth = jnp.maximum(wet, 1.0) / LEVELS
        ux = u / depth + raw[:, 2 + q, :]
        uy = v / depth + raw[:, 4 + q, :]
        drag = jnp.where(level < wet, raw[:, q, :] * jnp.sqrt(ux * ux + uy * uy), 0.0)
        for c, flow in enumerate((ux, uy)):
            product = drag * flow
            for h in range(2):
                share = jnp.where(low, product, 0.0) if h == 0 else jnp.where(low, 0.0, product)
                load = jnp.sum(share, axis=1, keepdims=True) / LEVELS
                result = jnp.where(lane == c * HELD + 2 * q + h, load, result)
    result = jnp.concatenate([result, jnp.zeros((128 - N_GY, 128), jnp.float32)], axis=0)
    rows = jnp.transpose(result)
    out = []
    for c in range(2):
        line = jnp.concatenate(
            [rows[c * HELD + i : c * HELD + i + 1, :N_GY] for i in range(HELD)], axis=1
        )
        out += [line[:, q * 128 : (q + 1) * 128] for q in range(3)]
    out.append(jnp.zeros((2, 128), jnp.float32))
    block = jnp.concatenate(out, axis=0)
    for j in range(N_GX):
        slots[j] = block


def inside_of(gy, gx):
    row = iota((EXT, WIDE), 0)
    lane = iota((EXT, WIDE), 1)
    inside = ((row >= HALO) | (gy > 0)) & ((row < HALO + ROWS) | (gy < N_GY - 1))
    return inside & (
        (lane < COLS)
        | ((lane < COLS + HALO) & (gx < N_GX - 1))
        | ((lane >= WIDE - HALO) & (gx > 0))
    )


def half_step(e, u, v, rub, push, inside):
    spread = pltpu.roll(u, WIDE - 1, 1) - pltpu.roll(u, 1, 1)
    spread = spread + (pltpu.roll(v, EXT - 1, 0) - pltpu.roll(v, 1, 0))
    mid = jnp.where(inside, e - C_MASS * spread, 0.0)
    scale = 1.0 / (1.0 + rub * jnp.sqrt(u * u + v * v))
    slope_x = pltpu.roll(mid, WIDE - 1, 1) - pltpu.roll(mid, 1, 1)
    slope_y = pltpu.roll(mid, EXT - 1, 0) - pltpu.roll(mid, 1, 0)
    return mid, (u - push * slope_x) * scale, (v - push * slope_y) * scale, scale


def ready_for_steps(smap, cells, fields, up, down, gy, gx):
    from_west = cells[jnp.maximum(gx - 1, 0), :GROUP, :]
    from_east = cells[jnp.minimum(gx + 1, N_GX - 1), :GROUP, :]
    lane = iota((GROUP, 128), 1)

    def widened(f, ref):
        side = []
        for g in range(3):
            at = g * SPAN + f * HALO
            east = pltpu.roll(from_east, (-at) % 128, 1)
            west = pltpu.roll(from_west, (120 - at) % 128, 1)
            side.append(jnp.where(lane < HALO, east, jnp.where(lane >= 120, west, 0.0)))
        side = jnp.concatenate(side, axis=0)[:EXT]
        return jnp.concatenate([extended(f, ref, up, down), side], axis=1)

    e, u, v, fric, lev = [widened(f, ref) for f, ref in enumerate(fields)]
    inside = inside_of(gy, gx)
    e = jnp.where(inside, e, 0.0)
    u = jnp.where(inside, u, 0.0)
    v = jnp.where(inside, v, 0.0)
    depth = jnp.where(inside, lev / LEVELS, 1.0)
    rub = jnp.where(inside, FRIC_STEP * fric / (depth * depth), 1.0)
    push = C_MOMENTUM * depth
    mid, u, v, scale = half_step(e, u, v, rub, push, inside)
    ends = FIELDS * HALO
    ids = jnp.concatenate(
        [up[ends:, :128], column_of(smap[...].astype(jnp.float32))[:ROWS], down[ends:, :128]],
        axis=0,
    ).astype(jnp.int32)
    parents = jnp.concatenate(
        [cells[j, STRIP_ROW : STRIP_ROW + 5, :] for j in range(N_GX)]
        + [jnp.zeros((128 - 5 * N_GX, 128), jnp.float32)],
        axis=0,
    )
    source = iota((EXT, 128), 1)
    column = jnp.zeros((EXT, 128), jnp.int32)
    for step in range(1, N_GX):
        column = column + (source >= 5 * step).astype(jnp.int32)
    first = ((gy - 2 + source - 5 * column) * N_GX + column) * 3
    slot_lane = jnp.right_shift(jnp.bitwise_and(iota((128, 128), 1), 63), 3)
    bound = jnp.zeros((EXT, 128), jnp.float32)
    for j in range(3):
        held = (ids == first + j) & (source < 5 * N_GX)
        for piece in three_parts(jnp.where(slot_lane == j, parents, 0.0)):
            bound = bound + jnp.dot(
                held.astype(jnp.bfloat16),
                piece.astype(jnp.bfloat16),
                preferred_element_type=jnp.float32,
            )
    bound = bound + pltpu.roll(bound, 120, 1) + pltpu.roll(bound, 112, 1)

    return mid, u, v, scale, rub, push, bound, inside


def step_kernel(smap, code, loads, cells, *refs):
    *fields, up, down, out_eta, out_u, out_v, force, fringe = refs
    gy = lax.axis_index("gy")
    gx = lax.axis_index("gx")
    for start in range(0, PLAT, CHUNK):
        tile_y, tile_x, row, col = decode(code[:, start : start + CHUNK])
        place = (tile_y - gy) * ROWS + row + HALO
        mine = iota((EXT, CHUNK), 0) == place
        across = (tile_x - gx) * COLS + col
        beside = jnp.where(across < 0, across + 2 * HALO, across - COLS)
        beside = jnp.where((across >= -HALO) & (across < COLS + HALO), beside, -1)
        right = (iota((COLS, CHUNK), 0) == across).astype(jnp.bfloat16)
        edge = iota((2 * HALO, CHUNK), 0) == beside
        left = []
        side = []
        for c in range(2):
            line = jnp.concatenate(
                [
                    loads[b // 3, 3 * c + b % 3 : 3 * c + b % 3 + 1, :]
                    for b in range(start // 128, (start + CHUNK) // 128)
                ],
                axis=1,
            )
            for part in three_parts(line)[:PARTS]:
                left.append(jnp.where(mine, part, 0.0))
                side.append(jnp.where(edge, part, 0.0))
        side.append(jnp.zeros((128 - 2 * HALO * len(side), CHUNK), jnp.float32))
        left = jnp.concatenate(left, axis=0).astype(jnp.bfloat16)
        side = jnp.concatenate(side, axis=0).astype(jnp.bfloat16)
        dims = (((1,), (1,)), ((), ()))
        inner = lax.dot_general(left, right, dims, preferred_element_type=jnp.float32)
        outer = lax.dot_general(
            mine.astype(jnp.bfloat16), side, dims, preferred_element_type=jnp.float32
        )
        if start == 0:
            force[...] = inner
            fringe[...] = outer
        else:
            force[...] += inner
            fringe[...] += outer
    lane = iota((EXT, 128), 1)
    sides = fringe[...]
    forces = []
    for c in range(2):
        inner = force[c * PARTS * EXT : (c * PARTS + 1) * EXT, :]
        at = 2 * HALO * PARTS * c
        outer = pltpu.roll(sides, (-at) % 128, 1)
        for n in range(1, PARTS):
            inner = inner + force[(c * PARTS + n) * EXT : (c * PARTS + n + 1) * EXT, :]
            outer = outer + pltpu.roll(sides, (-at - 2 * HALO * n) % 128, 1)
        west = pltpu.roll(outer, 128 - 2 * HALO, 1)
        outer = jnp.where(lane < HALO, outer, jnp.where(lane >= 128 - HALO, west, 0.0))
        forces.append(LOAD_GAIN * jnp.concatenate([inner, outer], axis=1))
    force_x, force_y = forces

    mid, flow_u, flow_v, scale, rub, push, bound, inside = ready_for_steps(
        smap, cells, fields, up, down, gy, gx
    )
    side_lane = iota((EXT, 128), 1)
    at_west = (side_lane == 0) & (gx == 0)
    at_east = (side_lane == 127) & (gx == N_GX - 1)
    root = FLATHER * jnp.sqrt(push[:, :COLS] * (1.0 / C_MOMENTUM))

    def finish(step, mid, u, v):
        sea, flow = [bound[:, 4 * f + step : 4 * f + step + 1] for f in range(2)]
        west = flow - root[:, :128] * (mid[:, :128] - sea)
        sea, flow = [bound[:, 64 + 4 * f + step : 64 + 4 * f + step + 1] for f in range(2)]
        east = flow + root[:, 128:] * (mid[:, 128:COLS] - sea)
        u = jnp.concatenate(
            [
                jnp.where(at_west, west, u[:, :128]),
                jnp.where(at_east, east, u[:, 128:COLS]),
                u[:, COLS:],
            ],
            axis=1,
        )
        return jnp.where(inside, u, 0.0), jnp.where(inside, v, 0.0)

    e = mid
    u, v = finish(0, e, flow_u - force_x * scale, flow_v - force_y * scale)
    for step in range(1, SUBSTEPS):
        e, u, v, s = half_step(e, u, v, rub, push, inside)
        u, v = finish(step, e, u - force_x * s, v - force_y * s)
    out_eta[...] = e[HALO : HALO + ROWS, :COLS]
    out_u[...] = u[HALO : HALO + ROWS, :COLS]
    out_v[...] = v[HALO : HALO + ROWS, :COLS]


def call(kernel, out_shape, spaces, name, scratch=(), limit=12, cycles=1, **kw):
    many = isinstance(out_shape, list)
    out_spec = pl.BlockSpec(memory_space=pltpu.VMEM)
    return pl.pallas_call(
        kernel,
        out_shape=out_shape,
        in_specs=[pl.BlockSpec(memory_space=space) for space in spaces],
        out_specs=[out_spec] * len(out_shape) if many else out_spec,
        scratch_shapes=list(scratch),
        compiler_params=pltpu.CompilerParams(vmem_limit_bytes=limit * 1024 * 1024),
        cost_estimate=pl.CostEstimate(
            flops=cycles * 10**8, bytes_accessed=cycles * 2 * 10**6, transcendentals=0
        ),
        name=name,
        **kw,
    )


def f32(*shape):
    return jax.ShapeDtypeStruct(shape, jnp.float32)


def on_device(
    sea_level,
    transport_x,
    transport_y,
    friction,
    levels,
    strip_map,
    parent_strip,
    plat_tile,
    plat_row,
    plat_col,
    plat_drag,
    plat_shear,
):
    fields = (sea_level, transport_x, transport_y, friction, levels)
    smap = strip_map.reshape(1, ROWS)
    vmem, hbm = pltpu.VMEM, pltpu.HBM
    sems = pltpu.SemaphoreType.DMA

    held = call(
        raw_kernel,
        f32(N_GY, 6, 128),
        [hbm] * 3,
        "raw",
        [
            pltpu.VMEM((HELD, LEVELS), jnp.float32),
            pltpu.VMEM((2, HELD, LEVELS), jnp.float32),
            pltpu.VMEM((2, 3, 2, SUBSTEPS), jnp.float32),
            sems((3,)),
        ],
        60,
    )(plat_drag.T, plat_shear.transpose(0, 2, 1), parent_strip.transpose(0, 3, 2, 1))
    raw = lax.all_to_all(held, "gy", 0, 0, tiled=True)

    top, bottom = call(
        row_halo_kernel, [f32(GROUP, COLS), f32(GROUP, COLS)], [vmem] * 6, "row_halo"
    )(*fields, smap)
    count = lax.axis_size("gy")
    upward = [(i, i + 1) for i in range(count - 1)]
    downward = [(target, source) for source, target in upward]
    near = (*fields, lax.ppermute(bottom, "gy", upward), lax.ppermute(top, "gy", downward))

    code = (plat_tile << 15) | (plat_row << 8) | plat_col
    code = code.reshape(N_GY, N_GX, HELD).transpose(1, 2, 0).reshape(1, PLAT)
    slots = call(
        cell_kernel,
        f32(N_GX, SLOT_ROWS, 128),
        [vmem] * 8,
        "cells",
        cycles=4,
    )(code, *near)
    slots = call(
        strip_kernel,
        f32(N_GX, SLOT_ROWS, 128),
        [vmem, vmem],
        "strips",
        input_output_aliases={1: 0},
    )(raw, slots)
    cells = lax.all_to_all(slots, "gx", 0, 0, tiled=True)
    slots = call(load_kernel, f32(N_GX, BACK_ROWS, 128), [vmem, vmem], "loads")(cells, raw)
    loads = lax.all_to_all(slots, "gx", 0, 0, tiled=True)
    out = f32(ROWS, COLS)
    force = [
        pltpu.VMEM((2 * PARTS * EXT, COLS), jnp.float32),
        pltpu.VMEM((EXT, 128), jnp.float32),
    ]
    return tuple(
        call(step_kernel, [out, out, out], [vmem] * 11, "steps", force)(
            smap, code, loads, cells, *near
        )
    )


def solution(mesh):
    return jax.shard_map(
        on_device,
        mesh=mesh,
        in_specs=(
            P("gy", "gx"),
            P("gy", "gx"),
            P("gy", "gx"),
            P("gy", "gx"),
            P("gy", "gx"),
            P("gy"),
            P(None, None, None, ("gy", "gx")),
            P(),
            P(),
            P(),
            P(None, ("gy", "gx")),
            P(None, None, ("gy", "gx")),
        ),
        out_specs=(P("gy", "gx"), P("gy", "gx"), P("gy", "gx")),
        check_vma=False,
    )
```

```python
import functools

import jax
import jax.numpy as jnp
from jax import lax
from jax.experimental import pallas as pl
from jax.experimental.pallas import tpu as pltpu
from jax.sharding import PartitionSpec as P

SUBSTEPS = 4
LEVELS = 60

C_MASS = 0.5
C_MOMENTUM = 0.8
FRIC_STEP = 0.5
LOAD_GAIN = 0.5
FLATHER = 0.7

ROWS = 120
COLS = 256
N_GX = 8
N_GY = 96
HELD = 4
PLAT = N_GY * N_GX * HELD
COL_PLAT = N_GY * HELD

HALO = 2 * SUBSTEPS
EXT = ROWS + 2 * HALO
WIDE = COLS + 128
GROUP = 48
FIELDS = 5
SPAN = FIELDS * HALO
CELL_ROW = GROUP
STRIP_ROW = GROUP + 9
SLOT_ROWS = 64
BACK_ROWS = 8
CHUNK = 512
FIRST_ROW = 68
FIRST_COL = 5
ROW_GROUP = [[(n + FIRST_ROW) % N_GY for n in range(N_GY)]]
COL_GROUP = [[(n + FIRST_COL) % N_GX for n in range(N_GX)]]
PARTS = 3


def iota(shape, dim):
    return lax.broadcasted_iota(jnp.int32, shape, dim)


def row_slot(gy):
    return lax.rem(gy + (N_GY - FIRST_ROW), N_GY)


def col_slot(gx):
    gx = gx + (N_GX - FIRST_COL)
    return gx % N_GX if isinstance(gx, int) else lax.rem(gx, N_GX)


def three_parts(x):
    high = x.astype(jnp.bfloat16).astype(jnp.float32)
    rest = x - high
    middle = rest.astype(jnp.bfloat16).astype(jnp.float32)
    return [high, middle, rest - middle]


def decode(code):
    col = jnp.bitwise_and(code, COLS - 1)
    row = jnp.bitwise_and(jnp.right_shift(code, 8), 127)
    tile_x = jnp.bitwise_and(jnp.right_shift(code, 15), N_GX - 1)
    tile_y = jnp.right_shift(code, 18)
    return tile_y, tile_x, row, col


def column_of(row_vector):
    row_vector = jnp.concatenate([row_vector, jnp.zeros((1, 128 - ROWS), jnp.float32)], axis=1)
    return jnp.transpose(jnp.broadcast_to(row_vector, (128, 128)))


def fetch(pairs, sems):
    copies = [pltpu.make_async_copy(src, dst, sems.at[n]) for n, (src, dst) in enumerate(pairs)]
    for copy in copies:
        copy.start()
    return copies


def raw_kernel(drag_in, shear_in, strip_in, slots, drag, shear, strip, sems):
    pairs = ((drag_in, drag), (shear_in, shear), (strip_in, strip))
    for copy in fetch(pairs, sems):
        copy.wait()
    held = (drag[...], shear[0], shear[1])
    lines = []
    for t in range(6):
        pieces = []
        for h in range(2):
            i = 2 * (t % 2) + h
            pieces.append(held[t // 2][i : i + 1, :])
            pieces.append(strip[h, t // 2][t % 2 : t % 2 + 1, :])
        lines.append(jnp.concatenate(pieces, axis=1))
    block = jnp.concatenate(lines, axis=0)
    for j in range(N_GY):
        slots[j] = block


def row_halo_kernel(eta, flow_u, flow_v, friction, levels, smap, top, bottom):
    last = ROWS - HALO
    for f, ref in enumerate((eta, flow_u, flow_v, friction, levels)):
        part = slice(f * HALO, (f + 1) * HALO)
        top[part, :] = ref[:HALO, :].astype(jnp.float32)
        bottom[part, :] = ref[last:, :].astype(jnp.float32)
    column = column_of(smap[...].astype(jnp.float32))
    for half in (slice(0, 128), slice(128, 256)):
        top[FIELDS * HALO :, half] = column[:HALO]
        bottom[FIELDS * HALO :, half] = column[last:ROWS]


def extended(f, ref, up, down):
    part = slice(f * HALO, (f + 1) * HALO)
    return jnp.concatenate([up[part, :], ref[...].astype(jnp.float32), down[part, :]], axis=0)


def cell_kernel(code, *refs):
    *fields, up, down, slots = refs
    gy = lax.axis_index("gy")
    gx = lax.axis_index("gx")
    wide = [extended(f, ref, up, down) for f, ref in enumerate(fields)]
    stack = three_parts(wide[1]) + three_parts(wide[2]) + [wide[4]]
    stack.append(jnp.zeros((HALO, COLS), jnp.float32))
    table = jnp.concatenate(stack, axis=0).astype(jnp.bfloat16)
    for start in range(0, PLAT, CHUNK):
        tile_y, tile_x, row, col = decode(code[:, start : start + CHUNK])
        place = (tile_y - gy) * ROWS + row + HALO
        near = (tile_x == gx) & (place >= 0) & (place < EXT)
        hot = iota((COLS, CHUNK), 0) == jnp.where(near, col, -1)
        found = jnp.dot(
            table, hot.astype(jnp.bfloat16), preferred_element_type=jnp.float32
        )
        mine = iota((EXT, CHUNK), 0) == place
        parts = [found[n * EXT : (n + 1) * EXT] for n in range(7)]
        values = [
            parts[0] + parts[1] + parts[2],
            parts[3] + parts[4] + parts[5],
            parts[6],
        ]
        for f, value in enumerate(values):
            line = jnp.sum(jnp.where(mine, value, 0.0), axis=0, keepdims=True)
            for b in range(CHUNK // 128):
                block = start // 128 + b
                r = CELL_ROW + 3 * f + block % 3
                slots[col_slot(block // 3), r : r + 1, :] = line[:, b * 128 : (b + 1) * 128]
    lane = iota((GROUP, 128), 1)
    west = jnp.zeros((GROUP, 128), jnp.float32)
    east = jnp.zeros((GROUP, 128), jnp.float32)
    for f in range(FIELDS):
        tall = jnp.concatenate(
            [wide[f], jnp.zeros((3 * GROUP - EXT, COLS), jnp.float32)], axis=0
        )
        for g in range(3):
            at = g * SPAN + f * HALO
            rows = slice(g * GROUP, (g + 1) * GROUP)
            mask = (lane >= at) & (lane < at + HALO)
            moved = pltpu.roll(tall[rows, :128], at, 1)
            west = jnp.where(mask, moved, west)
            moved = pltpu.roll(tall[rows, 128:], (at + HALO) % 128, 1)
            east = jnp.where(mask, moved, east)
    for j in range(N_GX):
        slots[col_slot(j), :GROUP, :] = jnp.where(j > gx, east, west)
    for j in range(N_GX):
        slots[j, CELL_ROW + 9 :, :] = jnp.zeros((SLOT_ROWS - CELL_ROW - 9, 128), jnp.float32)


def strip_kernel(raw, slots_in, slots):
    gy = lax.axis_index("gy")
    blocks = [raw[row_slot(jnp.clip(gy - 2 + b, 0, N_GY - 1))] for b in range(5)]
    lane = iota((8, 128), 1)
    group = jnp.right_shift(jnp.bitwise_and(lane, 63), 2)
    strip = jnp.zeros((8, 128), jnp.float32)
    for t in range(6):
        lines = [block[t : t + 1, :] for block in blocks] + [jnp.zeros((3, 128), jnp.float32)]
        moved = pltpu.roll(jnp.concatenate(lines, axis=0), (4 * t - LEVELS) % 128, 1)
        strip = jnp.where(group == t, moved, strip)
    for j in range(N_GX):
        slots[j, STRIP_ROW : STRIP_ROW + 5, :] = strip[:5]


def load_kernel(cells, raw, slots):
    total = cells[0, CELL_ROW : CELL_ROW + 9, :]
    for j in range(1, N_GX):
        total = total + cells[j, CELL_ROW : CELL_ROW + 9, :]
    lines = []
    for f in range(3):
        line = jnp.concatenate([total[3 * f + q : 3 * f + q + 1, :] for q in range(3)], axis=1)
        for i in range(HELD):
            part = line[:, i * N_GY : (i + 1) * N_GY]
            lines.append(
                jnp.concatenate([part, jnp.zeros((1, 128 - N_GY), jnp.float32)], axis=1)
            )
    lines.append(jnp.zeros((128 - len(lines), 128), jnp.float32))
    columns = jnp.transpose(jnp.concatenate(lines, axis=0))[:N_GY]
    lane = iota((N_GY, 128), 1)
    low = lane < 64
    level = jnp.bitwise_and(lane, 63).astype(jnp.float32)
    result = jnp.zeros((N_GY, 128), jnp.float32)
    for q in range(2):
        u, v, wet = [
            jnp.where(
                low,
                columns[:, f * HELD + 2 * q : f * HELD + 2 * q + 1],
                columns[:, f * HELD + 2 * q + 1 : f * HELD + 2 * q + 2],
            )
            for f in range(3)
        ]
        depth = jnp.maximum(wet, 1.0) / LEVELS
        ux = u / depth + raw[:, 2 + q, :]
        uy = v / depth + raw[:, 4 + q, :]
        drag = jnp.where(level < wet, raw[:, q, :] * jnp.sqrt(ux * ux + uy * uy), 0.0)
        for c, flow in enumerate((ux, uy)):
            product = drag * flow
            for h in range(2):
                share = jnp.where(low, product, 0.0) if h == 0 else jnp.where(low, 0.0, product)
                load = jnp.sum(share, axis=1, keepdims=True) / LEVELS
                result = jnp.where(lane == c * HELD + 2 * q + h, load, result)
    result = jnp.concatenate([result, jnp.zeros((128 - N_GY, 128), jnp.float32)], axis=0)
    rows = jnp.transpose(result)
    out = []
    for c in range(2):
        line = jnp.concatenate(
            [rows[c * HELD + i : c * HELD + i + 1, :N_GY] for i in range(HELD)], axis=1
        )
        out += [line[:, q * 128 : (q + 1) * 128] for q in range(3)]
    out.append(jnp.zeros((2, 128), jnp.float32))
    block = jnp.concatenate(out, axis=0)
    for j in range(N_GX):
        slots[j] = block


def inside_of(gy, gx):
    row = iota((EXT, WIDE), 0)
    lane = iota((EXT, WIDE), 1)
    inside = ((row >= HALO) | (gy > 0)) & ((row < HALO + ROWS) | (gy < N_GY - 1))
    return inside & (
        (lane < COLS)
        | ((lane < COLS + HALO) & (gx < N_GX - 1))
        | ((lane >= WIDE - HALO) & (gx > 0))
    )


def half_step(e, u, v, rub, push, inside):
    spread = pltpu.roll(u, WIDE - 1, 1) - pltpu.roll(u, 1, 1)
    spread = spread + (pltpu.roll(v, EXT - 1, 0) - pltpu.roll(v, 1, 0))
    mid = jnp.where(inside, e - C_MASS * spread, 0.0)
    scale = 1.0 / (1.0 + rub * jnp.sqrt(u * u + v * v))
    slope_x = pltpu.roll(mid, WIDE - 1, 1) - pltpu.roll(mid, 1, 1)
    slope_y = pltpu.roll(mid, EXT - 1, 0) - pltpu.roll(mid, 1, 0)
    return mid, (u - push * slope_x) * scale, (v - push * slope_y) * scale, scale


def ready_for_steps(smap, cells, fields, up, down, gy, gx):
    from_west = cells[col_slot(jnp.maximum(gx - 1, 0)), :GROUP, :]
    from_east = cells[col_slot(jnp.minimum(gx + 1, N_GX - 1)), :GROUP, :]
    lane = iota((GROUP, 128), 1)

    def widened(f, ref):
        side = []
        for g in range(3):
            at = g * SPAN + f * HALO
            east = pltpu.roll(from_east, (-at) % 128, 1)
            west = pltpu.roll(from_west, (120 - at) % 128, 1)
            side.append(jnp.where(lane < HALO, east, jnp.where(lane >= 120, west, 0.0)))
        side = jnp.concatenate(side, axis=0)[:EXT]
        return jnp.concatenate([extended(f, ref, up, down), side], axis=1)

    e, u, v, fric, lev = [widened(f, ref) for f, ref in enumerate(fields)]
    inside = inside_of(gy, gx)
    e = jnp.where(inside, e, 0.0)
    u = jnp.where(inside, u, 0.0)
    v = jnp.where(inside, v, 0.0)
    depth = jnp.where(inside, lev / LEVELS, 1.0)
    rub = jnp.where(inside, FRIC_STEP * fric / (depth * depth), 1.0)
    push = C_MOMENTUM * depth
    mid, u, v, scale = half_step(e, u, v, rub, push, inside)
    ends = FIELDS * HALO
    ids = jnp.concatenate(
        [up[ends:, :128], column_of(smap[...].astype(jnp.float32))[:ROWS], down[ends:, :128]],
        axis=0,
    ).astype(jnp.int32)
    parents = jnp.concatenate(
        [cells[col_slot(j), STRIP_ROW : STRIP_ROW + 5, :] for j in range(N_GX)]
        + [jnp.zeros((128 - 5 * N_GX, 128), jnp.float32)],
        axis=0,
    )
    source = iota((EXT, 128), 1)
    column = jnp.zeros((EXT, 128), jnp.int32)
    for step in range(1, N_GX):
        column = column + (source >= 5 * step).astype(jnp.int32)
    first = ((gy - 2 + source - 5 * column) * N_GX + column) * 3
    slot_lane = jnp.right_shift(jnp.bitwise_and(iota((128, 128), 1), 63), 3)
    bound = jnp.zeros((EXT, 128), jnp.float32)
    for j in range(3):
        held = (ids == first + j) & (source < 5 * N_GX)
        for piece in three_parts(jnp.where(slot_lane == j, parents, 0.0)):
            bound = bound + jnp.dot(
                held.astype(jnp.bfloat16),
                piece.astype(jnp.bfloat16),
                preferred_element_type=jnp.float32,
            )
    bound = bound + pltpu.roll(bound, 120, 1) + pltpu.roll(bound, 112, 1)

    return mid, u, v, scale, rub, push, bound, inside


def step_kernel(smap, code, loads, cells, *refs):
    *fields, up, down, out_eta, out_u, out_v, force, fringe = refs
    gy = lax.axis_index("gy")
    gx = lax.axis_index("gx")
    for start in range(0, PLAT, CHUNK):
        tile_y, tile_x, row, col = decode(code[:, start : start + CHUNK])
        place = (tile_y - gy) * ROWS + row + HALO
        mine = iota((EXT, CHUNK), 0) == place
        across = (tile_x - gx) * COLS + col
        beside = jnp.where(across < 0, across + 2 * HALO, across - COLS)
        beside = jnp.where((across >= -HALO) & (across < COLS + HALO), beside, -1)
        right = (iota((COLS, CHUNK), 0) == across).astype(jnp.bfloat16)
        edge = iota((2 * HALO, CHUNK), 0) == beside
        left = []
        side = []
        for c in range(2):
            line = jnp.concatenate(
                [
                    loads[col_slot(b // 3), 3 * c + b % 3 : 3 * c + b % 3 + 1, :]
                    for b in range(start // 128, (start + CHUNK) // 128)
                ],
                axis=1,
            )
            for part in three_parts(line)[:PARTS]:
                left.append(jnp.where(mine, part, 0.0))
                side.append(jnp.where(edge, part, 0.0))
        side.append(jnp.zeros((128 - 2 * HALO * len(side), CHUNK), jnp.float32))
        left = jnp.concatenate(left, axis=0).astype(jnp.bfloat16)
        side = jnp.concatenate(side, axis=0).astype(jnp.bfloat16)
        dims = (((1,), (1,)), ((), ()))
        inner = lax.dot_general(left, right, dims, preferred_element_type=jnp.float32)
        outer = lax.dot_general(
            mine.astype(jnp.bfloat16), side, dims, preferred_element_type=jnp.float32
        )
        if start == 0:
            force[...] = inner
            fringe[...] = outer
        else:
            force[...] += inner
            fringe[...] += outer
    lane = iota((EXT, 128), 1)
    sides = fringe[...]
    forces = []
    for c in range(2):
        inner = force[c * PARTS * EXT : (c * PARTS + 1) * EXT, :]
        at = 2 * HALO * PARTS * c
        outer = pltpu.roll(sides, (-at) % 128, 1)
        for n in range(1, PARTS):
            inner = inner + force[(c * PARTS + n) * EXT : (c * PARTS + n + 1) * EXT, :]
            outer = outer + pltpu.roll(sides, (-at - 2 * HALO * n) % 128, 1)
        west = pltpu.roll(outer, 128 - 2 * HALO, 1)
        outer = jnp.where(lane < HALO, outer, jnp.where(lane >= 128 - HALO, west, 0.0))
        forces.append(LOAD_GAIN * jnp.concatenate([inner, outer], axis=1))
    force_x, force_y = forces

    mid, flow_u, flow_v, scale, rub, push, bound, inside = ready_for_steps(
        smap, cells, fields, up, down, gy, gx
    )
    side_lane = iota((EXT, 128), 1)
    at_west = (side_lane == 0) & (gx == 0)
    at_east = (side_lane == 127) & (gx == N_GX - 1)
    root = FLATHER * jnp.sqrt(push[:, :COLS] * (1.0 / C_MOMENTUM))

    def finish(step, mid, u, v):
        sea, flow = [bound[:, 4 * f + step : 4 * f + step + 1] for f in range(2)]
        west = flow - root[:, :128] * (mid[:, :128] - sea)
        sea, flow = [bound[:, 64 + 4 * f + step : 64 + 4 * f + step + 1] for f in range(2)]
        east = flow + root[:, 128:] * (mid[:, 128:COLS] - sea)
        u = jnp.concatenate(
            [
                jnp.where(at_west, west, u[:, :128]),
                jnp.where(at_east, east, u[:, 128:COLS]),
                u[:, COLS:],
            ],
            axis=1,
        )
        return jnp.where(inside, u, 0.0), jnp.where(inside, v, 0.0)

    e = mid
    u, v = finish(0, e, flow_u - force_x * scale, flow_v - force_y * scale)
    for step in range(1, SUBSTEPS):
        e, u, v, s = half_step(e, u, v, rub, push, inside)
        u, v = finish(step, e, u - force_x * s, v - force_y * s)
    out_eta[...] = e[HALO : HALO + ROWS, :COLS]
    out_u[...] = u[HALO : HALO + ROWS, :COLS]
    out_v[...] = v[HALO : HALO + ROWS, :COLS]


def call(kernel, out_shape, spaces, name, scratch=(), limit=12, cycles=1, **kw):
    many = isinstance(out_shape, list)
    out_spec = pl.BlockSpec(memory_space=pltpu.VMEM)
    return pl.pallas_call(
        kernel,
        out_shape=out_shape,
        in_specs=[pl.BlockSpec(memory_space=space) for space in spaces],
        out_specs=[out_spec] * len(out_shape) if many else out_spec,
        scratch_shapes=list(scratch),
        compiler_params=pltpu.CompilerParams(vmem_limit_bytes=limit * 1024 * 1024),
        cost_estimate=pl.CostEstimate(
            flops=cycles * 10**8, bytes_accessed=cycles * 2 * 10**6, transcendentals=0
        ),
        name=name,
        **kw,
    )


def f32(*shape):
    return jax.ShapeDtypeStruct(shape, jnp.float32)


def on_device(
    sea_level,
    transport_x,
    transport_y,
    friction,
    levels,
    strip_map,
    parent_strip,
    plat_tile,
    plat_row,
    plat_col,
    plat_drag,
    plat_shear,
):
    fields = (sea_level, transport_x, transport_y, friction, levels)
    smap = strip_map.reshape(1, ROWS)
    vmem, hbm = pltpu.VMEM, pltpu.HBM
    sems = pltpu.SemaphoreType.DMA

    held = call(
        raw_kernel,
        f32(N_GY, 6, 128),
        [hbm] * 3,
        "raw",
        [
            pltpu.VMEM((HELD, LEVELS), jnp.float32),
            pltpu.VMEM((2, HELD, LEVELS), jnp.float32),
            pltpu.VMEM((2, 3, 2, SUBSTEPS), jnp.float32),
            sems((3,)),
        ],
        60,
    )(plat_drag.T, plat_shear.transpose(0, 2, 1), parent_strip.transpose(0, 3, 2, 1))
    raw = lax.all_to_all(
        held, "gy", 0, 0, axis_index_groups=ROW_GROUP, tiled=True
    )

    top, bottom = call(
        row_halo_kernel, [f32(GROUP, COLS), f32(GROUP, COLS)], [vmem] * 6, "row_halo"
    )(*fields, smap)
    count = lax.axis_size("gy")
    upward = [(i, i + 1) for i in range(count - 1)]
    downward = [(target, source) for source, target in upward]
    near = (*fields, lax.ppermute(bottom, "gy", upward), lax.ppermute(top, "gy", downward))

    code = (plat_tile << 15) | (plat_row << 8) | plat_col
    start = FIRST_ROW * N_GX * HELD
    code = jnp.concatenate([code[start:], code[:start]]).reshape(N_GY, N_GX, HELD).transpose(1, 2, 0).reshape(1, PLAT)
    slots = call(
        cell_kernel,
        f32(N_GX, SLOT_ROWS, 128),
        [vmem] * 8,
        "cells",
        cycles=4,
    )(code, *near)
    slots = call(
        strip_kernel,
        f32(N_GX, SLOT_ROWS, 128),
        [vmem, vmem],
        "strips",
        input_output_aliases={1: 0},
    )(raw, slots)
    cells = lax.all_to_all(slots, "gx", 0, 0, axis_index_groups=COL_GROUP, tiled=True)
    slots = call(load_kernel, f32(N_GX, BACK_ROWS, 128), [vmem, vmem], "loads")(cells, raw)
    loads = lax.all_to_all(slots, "gx", 0, 0, axis_index_groups=COL_GROUP, tiled=True)
    out = f32(ROWS, COLS)
    force = [
        pltpu.VMEM((2 * PARTS * EXT, COLS), jnp.float32),
        pltpu.VMEM((EXT, 128), jnp.float32),
    ]
    return tuple(
        call(step_kernel, [out, out, out], [vmem] * 11, "steps", force)(
            smap, code, loads, cells, *near
        )
    )


def solution(mesh):
    return jax.shard_map(
        on_device,
        mesh=mesh,
        in_specs=(
            P("gy", "gx"),
            P("gy", "gx"),
            P("gy", "gx"),
            P("gy", "gx"),
            P("gy", "gx"),
            P("gy"),
            P(None, None, None, ("gy", "gx")),
            P(),
            P(),
            P(),
            P(None, ("gy", "gx")),
            P(None, None, ("gy", "gx")),
        ),
        out_specs=(P("gy", "gx"), P("gy", "gx"), P("gy", "gx")),
        check_vma=False,
    )
```

```python
import functools

import jax
import jax.numpy as jnp
from jax import lax
from jax.experimental import pallas as pl
from jax.experimental.pallas import tpu as pltpu
from jax.sharding import PartitionSpec as P

SUBSTEPS = 4
LEVELS = 60

C_MASS = 0.5
C_MOMENTUM = 0.8
FRIC_STEP = 0.5
LOAD_GAIN = 0.5
FLATHER = 0.7

ROWS = 120
COLS = 256
N_GX = 8
N_GY = 96
HELD = 4
PLAT = N_GY * N_GX * HELD
COL_PLAT = N_GY * HELD

HALO = 2 * SUBSTEPS
EXT = ROWS + 2 * HALO
WIDE = COLS + 128
GROUP = 48
FIELDS = 5
SPAN = FIELDS * HALO
CELL_ROW = GROUP
STRIP_ROW = GROUP + 9
SLOT_ROWS = 64
BACK_ROWS = 8
CHUNK = 512
FIRST_ROW = 68
FIRST_COL = 5
ROW_GROUP = [[(n + FIRST_ROW) % N_GY for n in range(N_GY)]]
COL_GROUP = [[(n + FIRST_COL) % N_GX for n in range(N_GX)]]
PARTS = 2


def iota(shape, dim):
    return lax.broadcasted_iota(jnp.int32, shape, dim)


def row_slot(gy):
    return lax.rem(gy + (N_GY - FIRST_ROW), N_GY)


def col_slot(gx):
    gx = gx + (N_GX - FIRST_COL)
    return gx % N_GX if isinstance(gx, int) else lax.rem(gx, N_GX)


def three_parts(x):
    high = x.astype(jnp.bfloat16).astype(jnp.float32)
    rest = x - high
    middle = rest.astype(jnp.bfloat16).astype(jnp.float32)
    return [high, middle, rest - middle]


def decode(code):
    col = jnp.bitwise_and(code, COLS - 1)
    row = jnp.bitwise_and(jnp.right_shift(code, 8), 127)
    tile_x = jnp.bitwise_and(jnp.right_shift(code, 15), N_GX - 1)
    tile_y = jnp.right_shift(code, 18)
    return tile_y, tile_x, row, col


def column_of(row_vector):
    row_vector = jnp.concatenate([row_vector, jnp.zeros((1, 128 - ROWS), jnp.float32)], axis=1)
    return jnp.transpose(jnp.broadcast_to(row_vector, (128, 128)))


def fetch(pairs, sems):
    copies = [pltpu.make_async_copy(src, dst, sems.at[n]) for n, (src, dst) in enumerate(pairs)]
    for copy in copies:
        copy.start()
    return copies


def raw_kernel(drag_in, shear_in, strip_in, slots, drag, shear, strip, sems):
    pairs = ((drag_in, drag), (shear_in, shear), (strip_in, strip))
    for copy in fetch(pairs, sems):
        copy.wait()
    held = (drag[...], shear[0], shear[1])
    lines = []
    for t in range(6):
        pieces = []
        for h in range(2):
            i = 2 * (t % 2) + h
            pieces.append(held[t // 2][i : i + 1, :])
            pieces.append(strip[h, t // 2][t % 2 : t % 2 + 1, :])
        lines.append(jnp.concatenate(pieces, axis=1))
    block = jnp.concatenate(lines, axis=0)
    for j in range(N_GY):
        slots[j] = block


def row_halo_kernel(eta, flow_u, flow_v, friction, levels, smap, top, bottom):
    last = ROWS - HALO
    for f, ref in enumerate((eta, flow_u, flow_v, friction, levels)):
        part = slice(f * HALO, (f + 1) * HALO)
        top[part, :] = ref[:HALO, :].astype(jnp.float32)
        bottom[part, :] = ref[last:, :].astype(jnp.float32)
    column = column_of(smap[...].astype(jnp.float32))
    for half in (slice(0, 128), slice(128, 256)):
        top[FIELDS * HALO :, half] = column[:HALO]
        bottom[FIELDS * HALO :, half] = column[last:ROWS]


def extended(f, ref, up, down):
    part = slice(f * HALO, (f + 1) * HALO)
    return jnp.concatenate([up[part, :], ref[...].astype(jnp.float32), down[part, :]], axis=0)


def cell_kernel(code, *refs):
    *fields, up, down, slots = refs
    gy = lax.axis_index("gy")
    gx = lax.axis_index("gx")
    wide = [extended(f, ref, up, down) for f, ref in enumerate(fields)]
    stack = three_parts(wide[1]) + three_parts(wide[2]) + [wide[4]]
    stack.append(jnp.zeros((HALO, COLS), jnp.float32))
    table = jnp.concatenate(stack, axis=0).astype(jnp.bfloat16)
    for start in range(0, PLAT, CHUNK):
        tile_y, tile_x, row, col = decode(code[:, start : start + CHUNK])
        place = (tile_y - gy) * ROWS + row + HALO
        near = (tile_x == gx) & (place >= 0) & (place < EXT)
        hot = iota((COLS, CHUNK), 0) == jnp.where(near, col, -1)
        found = jnp.dot(
            table, hot.astype(jnp.bfloat16), preferred_element_type=jnp.float32
        )
        mine = iota((EXT, CHUNK), 0) == place
        parts = [found[n * EXT : (n + 1) * EXT] for n in range(7)]
        values = [
            parts[0] + parts[1] + parts[2],
            parts[3] + parts[4] + parts[5],
            parts[6],
        ]
        for f, value in enumerate(values):
            line = jnp.sum(jnp.where(mine, value, 0.0), axis=0, keepdims=True)
            for b in range(CHUNK // 128):
                block = start // 128 + b
                r = CELL_ROW + 3 * f + block % 3
                slots[col_slot(block // 3), r : r + 1, :] = line[:, b * 128 : (b + 1) * 128]
    lane = iota((GROUP, 128), 1)
    west = jnp.zeros((GROUP, 128), jnp.float32)
    east = jnp.zeros((GROUP, 128), jnp.float32)
    for f in range(FIELDS):
        tall = jnp.concatenate(
            [wide[f], jnp.zeros((3 * GROUP - EXT, COLS), jnp.float32)], axis=0
        )
        for g in range(3):
            at = g * SPAN + f * HALO
            rows = slice(g * GROUP, (g + 1) * GROUP)
            mask = (lane >= at) & (lane < at + HALO)
            moved = pltpu.roll(tall[rows, :128], at, 1)
            west = jnp.where(mask, moved, west)
            moved = pltpu.roll(tall[rows, 128:], (at + HALO) % 128, 1)
            east = jnp.where(mask, moved, east)
    for j in range(N_GX):
        slots[col_slot(j), :GROUP, :] = jnp.where(j > gx, east, west)
    for j in range(N_GX):
        slots[j, CELL_ROW + 9 :, :] = jnp.zeros((SLOT_ROWS - CELL_ROW - 9, 128), jnp.float32)


def strip_kernel(raw, slots_in, slots):
    gy = lax.axis_index("gy")
    blocks = [raw[row_slot(jnp.clip(gy - 2 + b, 0, N_GY - 1))] for b in range(5)]
    lane = iota((8, 128), 1)
    group = jnp.right_shift(jnp.bitwise_and(lane, 63), 2)
    strip = jnp.zeros((8, 128), jnp.float32)
    for t in range(6):
        lines = [block[t : t + 1, :] for block in blocks] + [jnp.zeros((3, 128), jnp.float32)]
        moved = pltpu.roll(jnp.concatenate(lines, axis=0), (4 * t - LEVELS) % 128, 1)
        strip = jnp.where(group == t, moved, strip)
    for j in range(N_GX):
        slots[j, STRIP_ROW : STRIP_ROW + 5, :] = strip[:5]


def load_kernel(cells, raw, slots):
    total = cells[0, CELL_ROW : CELL_ROW + 9, :]
    for j in range(1, N_GX):
        total = total + cells[j, CELL_ROW : CELL_ROW + 9, :]
    lines = []
    for f in range(3):
        line = jnp.concatenate([total[3 * f + q : 3 * f + q + 1, :] for q in range(3)], axis=1)
        for i in range(HELD):
            part = line[:, i * N_GY : (i + 1) * N_GY]
            lines.append(
                jnp.concatenate([part, jnp.zeros((1, 128 - N_GY), jnp.float32)], axis=1)
            )
    lines.append(jnp.zeros((128 - len(lines), 128), jnp.float32))
    columns = jnp.transpose(jnp.concatenate(lines, axis=0))[:N_GY]
    lane = iota((N_GY, 128), 1)
    low = lane < 64
    level = jnp.bitwise_and(lane, 63).astype(jnp.float32)
    result = jnp.zeros((N_GY, 128), jnp.float32)
    for q in range(2):
        u, v, wet = [
            jnp.where(
                low,
                columns[:, f * HELD + 2 * q : f * HELD + 2 * q + 1],
                columns[:, f * HELD + 2 * q + 1 : f * HELD + 2 * q + 2],
            )
            for f in range(3)
        ]
        depth = jnp.maximum(wet, 1.0) / LEVELS
        ux = u / depth + raw[:, 2 + q, :]
        uy = v / depth + raw[:, 4 + q, :]
        drag = jnp.where(level < wet, raw[:, q, :] * jnp.sqrt(ux * ux + uy * uy), 0.0)
        for c, flow in enumerate((ux, uy)):
            product = drag * flow
            for h in range(2):
                share = jnp.where(low, product, 0.0) if h == 0 else jnp.where(low, 0.0, product)
                load = jnp.sum(share, axis=1, keepdims=True) / LEVELS
                result = jnp.where(lane == c * HELD + 2 * q + h, load, result)
    result = jnp.concatenate([result, jnp.zeros((128 - N_GY, 128), jnp.float32)], axis=0)
    rows = jnp.transpose(result)
    out = []
    for c in range(2):
        line = jnp.concatenate(
            [rows[c * HELD + i : c * HELD + i + 1, :N_GY] for i in range(HELD)], axis=1
        )
        out += [line[:, q * 128 : (q + 1) * 128] for q in range(3)]
    out.append(jnp.zeros((2, 128), jnp.float32))
    block = jnp.concatenate(out, axis=0)
    for j in range(N_GX):
        slots[j] = block


def inside_of(gy, gx):
    row = iota((EXT, WIDE), 0)
    lane = iota((EXT, WIDE), 1)
    inside = ((row >= HALO) | (gy > 0)) & ((row < HALO + ROWS) | (gy < N_GY - 1))
    return inside & (
        (lane < COLS)
        | ((lane < COLS + HALO) & (gx < N_GX - 1))
        | ((lane >= WIDE - HALO) & (gx > 0))
    )


def half_step(e, u, v, rub, push, inside, emit=None):
    spread = pltpu.roll(u, WIDE - 1, 1) - pltpu.roll(u, 1, 1)
    spread = spread + (pltpu.roll(v, EXT - 1, 0) - pltpu.roll(v, 1, 0))
    mid = jnp.where(inside, e - C_MASS * spread, 0.0)
    if emit is not None:
        emit(0, mid)
    scale = 1.0 / (1.0 + rub * jnp.sqrt(u * u + v * v))
    slope_x = pltpu.roll(mid, WIDE - 1, 1) - pltpu.roll(mid, 1, 1)
    slope_y = pltpu.roll(mid, EXT - 1, 0) - pltpu.roll(mid, 1, 0)
    return mid, (u - push * slope_x) * scale, (v - push * slope_y) * scale, scale


def ready_for_steps(smap, cells, fields, up, down, gy, gx):
    from_west = cells[col_slot(jnp.maximum(gx - 1, 0)), :GROUP, :]
    from_east = cells[col_slot(jnp.minimum(gx + 1, N_GX - 1)), :GROUP, :]
    lane = iota((GROUP, 128), 1)

    def widened(f, ref):
        side = []
        for g in range(3):
            at = g * SPAN + f * HALO
            east = pltpu.roll(from_east, (-at) % 128, 1)
            west = pltpu.roll(from_west, (120 - at) % 128, 1)
            side.append(jnp.where(lane < HALO, east, jnp.where(lane >= 120, west, 0.0)))
        side = jnp.concatenate(side, axis=0)[:EXT]
        return jnp.concatenate([extended(f, ref, up, down), side], axis=1)

    e, u, v, fric, lev = [widened(f, ref) for f, ref in enumerate(fields)]
    inside = inside_of(gy, gx)
    e = jnp.where(inside, e, 0.0)
    u = jnp.where(inside, u, 0.0)
    v = jnp.where(inside, v, 0.0)
    depth = jnp.where(inside, lev / LEVELS, 1.0)
    rub = jnp.where(inside, FRIC_STEP * fric / (depth * depth), 1.0)
    push = C_MOMENTUM * depth
    mid, u, v, scale = half_step(e, u, v, rub, push, inside)
    ends = FIELDS * HALO
    ids = jnp.concatenate(
        [up[ends:, :128], column_of(smap[...].astype(jnp.float32))[:ROWS], down[ends:, :128]],
        axis=0,
    ).astype(jnp.int32)
    parents = jnp.concatenate(
        [cells[col_slot(j), STRIP_ROW : STRIP_ROW + 5, :] for j in range(N_GX)]
        + [jnp.zeros((128 - 5 * N_GX, 128), jnp.float32)],
        axis=0,
    )
    source = iota((EXT, 128), 1)
    column = jnp.zeros((EXT, 128), jnp.int32)
    for step in range(1, N_GX):
        column = column + (source >= 5 * step).astype(jnp.int32)
    first = ((gy - 2 + source - 5 * column) * N_GX + column) * 3
    slot_lane = jnp.right_shift(jnp.bitwise_and(iota((128, 128), 1), 63), 3)
    bound = jnp.zeros((EXT, 128), jnp.float32)
    for j in range(3):
        held = (ids == first + j) & (source < 5 * N_GX)
        for piece in three_parts(jnp.where(slot_lane == j, parents, 0.0)):
            bound = bound + jnp.dot(
                held.astype(jnp.bfloat16),
                piece.astype(jnp.bfloat16),
                preferred_element_type=jnp.float32,
            )
    bound = bound + pltpu.roll(bound, 120, 1) + pltpu.roll(bound, 112, 1)

    return mid, u, v, scale, rub, push, bound, inside


def step_kernel(smap, code, loads, cells, *refs):
    *fields, up, down, out_eta, out_u, out_v, force, fringe, staged, sems = refs
    outs = (out_eta, out_u, out_v)

    def send(n, field):
        staged[n] = field[HALO : HALO + ROWS, :COLS]
        pltpu.make_async_copy(staged.at[n], outs[n], sems.at[n]).start()

    gy = lax.axis_index("gy")
    gx = lax.axis_index("gx")
    for start in range(0, PLAT, CHUNK):
        tile_y, tile_x, row, col = decode(code[:, start : start + CHUNK])
        place = (tile_y - gy) * ROWS + row + HALO
        mine = iota((EXT, CHUNK), 0) == place
        across = (tile_x - gx) * COLS + col
        beside = jnp.where(across < 0, across + 2 * HALO, across - COLS)
        beside = jnp.where((across >= -HALO) & (across < COLS + HALO), beside, -1)
        right = (iota((COLS, CHUNK), 0) == across).astype(jnp.bfloat16)
        edge = iota((2 * HALO, CHUNK), 0) == beside
        left = []
        side = []
        for c in range(2):
            line = jnp.concatenate(
                [
                    loads[col_slot(b // 3), 3 * c + b % 3 : 3 * c + b % 3 + 1, :]
                    for b in range(start // 128, (start + CHUNK) // 128)
                ],
                axis=1,
            )
            for part in three_parts(line)[:PARTS]:
                left.append(jnp.where(mine, part, 0.0))
                side.append(jnp.where(edge, part, 0.0))
        side.append(jnp.zeros((128 - 2 * HALO * len(side), CHUNK), jnp.float32))
        left = jnp.concatenate(left, axis=0).astype(jnp.bfloat16)
        side = jnp.concatenate(side, axis=0).astype(jnp.bfloat16)
        dims = (((1,), (1,)), ((), ()))
        inner = lax.dot_general(left, right, dims, preferred_element_type=jnp.float32)
        outer = lax.dot_general(
            mine.astype(jnp.bfloat16), side, dims, preferred_element_type=jnp.float32
        )
        if start == 0:
            force[...] = inner
            fringe[...] = outer
        else:
            force[...] += inner
            fringe[...] += outer
    lane = iota((EXT, 128), 1)
    sides = fringe[...]
    forces = []
    for c in range(2):
        inner = force[c * PARTS * EXT : (c * PARTS + 1) * EXT, :]
        at = 2 * HALO * PARTS * c
        outer = pltpu.roll(sides, (-at) % 128, 1)
        for n in range(1, PARTS):
            inner = inner + force[(c * PARTS + n) * EXT : (c * PARTS + n + 1) * EXT, :]
            outer = outer + pltpu.roll(sides, (-at - 2 * HALO * n) % 128, 1)
        west = pltpu.roll(outer, 128 - 2 * HALO, 1)
        outer = jnp.where(lane < HALO, outer, jnp.where(lane >= 128 - HALO, west, 0.0))
        forces.append(LOAD_GAIN * jnp.concatenate([inner, outer], axis=1))
    force_x, force_y = forces

    mid, flow_u, flow_v, scale, rub, push, bound, inside = ready_for_steps(
        smap, cells, fields, up, down, gy, gx
    )
    side_lane = iota((EXT, 128), 1)
    at_west = (side_lane == 0) & (gx == 0)
    at_east = (side_lane == 127) & (gx == N_GX - 1)
    root = FLATHER * jnp.sqrt(push[:, :COLS] * (1.0 / C_MOMENTUM))

    def finish(step, mid, u, v):
        sea, flow = [bound[:, 4 * f + step : 4 * f + step + 1] for f in range(2)]
        west = flow - root[:, :128] * (mid[:, :128] - sea)
        sea, flow = [bound[:, 64 + 4 * f + step : 64 + 4 * f + step + 1] for f in range(2)]
        east = flow + root[:, 128:] * (mid[:, 128:COLS] - sea)
        u = jnp.concatenate(
            [
                jnp.where(at_west, west, u[:, :128]),
                jnp.where(at_east, east, u[:, 128:COLS]),
                u[:, COLS:],
            ],
            axis=1,
        )
        u = jnp.where(inside, u, 0.0)
        if step == SUBSTEPS - 1:
            send(1, u)
        return u, jnp.where(inside, v, 0.0)

    e = mid
    u, v = finish(0, e, flow_u - force_x * scale, flow_v - force_y * scale)
    for step in range(1, SUBSTEPS):
        emit = send if step == SUBSTEPS - 1 else None
        e, u, v, s = half_step(e, u, v, rub, push, inside, emit)
        u, v = finish(step, e, u - force_x * s, v - force_y * s)
    send(2, v)
    for n in range(3):
        pltpu.make_async_copy(staged.at[n], outs[n], sems.at[n]).wait()


def call(
    kernel, out_shape, spaces, name, scratch=(), limit=12, cycles=1, out_space=pltpu.VMEM, **kw
):
    many = isinstance(out_shape, list)
    out_spec = pl.BlockSpec(memory_space=out_space)
    return pl.pallas_call(
        kernel,
        out_shape=out_shape,
        in_specs=[pl.BlockSpec(memory_space=space) for space in spaces],
        out_specs=[out_spec] * len(out_shape) if many else out_spec,
        scratch_shapes=list(scratch),
        compiler_params=pltpu.CompilerParams(vmem_limit_bytes=limit * 1024 * 1024),
        cost_estimate=pl.CostEstimate(
            flops=cycles * 10**8, bytes_accessed=cycles * 2 * 10**6, transcendentals=0
        ),
        name=name,
        **kw,
    )


def f32(*shape):
    return jax.ShapeDtypeStruct(shape, jnp.float32)


def on_device(
    sea_level,
    transport_x,
    transport_y,
    friction,
    levels,
    strip_map,
    parent_strip,
    plat_tile,
    plat_row,
    plat_col,
    plat_drag,
    plat_shear,
):
    fields = (sea_level, transport_x, transport_y, friction, levels)
    smap = strip_map.reshape(1, ROWS)
    vmem, hbm = pltpu.VMEM, pltpu.HBM
    sems = pltpu.SemaphoreType.DMA

    held = call(
        raw_kernel,
        f32(N_GY, 6, 128),
        [hbm] * 3,
        "raw",
        [
            pltpu.VMEM((HELD, LEVELS), jnp.float32),
            pltpu.VMEM((2, HELD, LEVELS), jnp.float32),
            pltpu.VMEM((2, 3, 2, SUBSTEPS), jnp.float32),
            sems((3,)),
        ],
        60,
    )(plat_drag.T, plat_shear.transpose(0, 2, 1), parent_strip.transpose(0, 3, 2, 1))
    raw = lax.all_to_all(
        held, "gy", 0, 0, axis_index_groups=ROW_GROUP, tiled=True
    )

    top, bottom = call(
        row_halo_kernel, [f32(GROUP, COLS), f32(GROUP, COLS)], [vmem] * 6, "row_halo"
    )(*fields, smap)
    count = lax.axis_size("gy")
    upward = [(i, i + 1) for i in range(count - 1)]
    downward = [(target, source) for source, target in upward]
    near = (*fields, lax.ppermute(bottom, "gy", upward), lax.ppermute(top, "gy", downward))

    code = (plat_tile << 15) | (plat_row << 8) | plat_col
    start = FIRST_ROW * N_GX * HELD
    code = jnp.concatenate([code[start:], code[:start]]).reshape(N_GY, N_GX, HELD).transpose(1, 2, 0).reshape(1, PLAT)
    slots = call(
        cell_kernel,
        f32(N_GX, SLOT_ROWS, 128),
        [vmem] * 8,
        "cells",
        cycles=4,
    )(code, *near)
    slots = call(
        strip_kernel,
        f32(N_GX, SLOT_ROWS, 128),
        [vmem, vmem],
        "strips",
        input_output_aliases={1: 0},
    )(raw, slots)
    cells = lax.all_to_all(slots, "gx", 0, 0, axis_index_groups=COL_GROUP, tiled=True)
    slots = call(load_kernel, f32(N_GX, BACK_ROWS, 128), [vmem, vmem], "loads")(cells, raw)
    loads = lax.all_to_all(slots, "gx", 0, 0, axis_index_groups=COL_GROUP, tiled=True)
    out = f32(ROWS, COLS)
    force = [
        pltpu.VMEM((2 * PARTS * EXT, COLS), jnp.float32),
        pltpu.VMEM((EXT, 128), jnp.float32),
        pltpu.VMEM((3, ROWS, COLS), jnp.float32),
        sems((3,)),
    ]
    return tuple(
        call(step_kernel, [out, out, out], [vmem] * 11, "steps", force, out_space=hbm)(
            smap, code, loads, cells, *near
        )
    )


def solution(mesh):
    return jax.shard_map(
        on_device,
        mesh=mesh,
        in_specs=(
            P("gy", "gx"),
            P("gy", "gx"),
            P("gy", "gx"),
            P("gy", "gx"),
            P("gy", "gx"),
            P("gy"),
            P(None, None, None, ("gy", "gx")),
            P(),
            P(),
            P(),
            P(None, ("gy", "gx")),
            P(None, None, ("gy", "gx")),
        ),
        out_specs=(P("gy", "gx"), P("gy", "gx"), P("gy", "gx")),
        check_vma=False,
    )
```

```python
import functools

import jax
import jax.numpy as jnp
from jax import lax
from jax.experimental import pallas as pl
from jax.experimental.pallas import tpu as pltpu
from jax.sharding import PartitionSpec as P

SUBSTEPS = 4
LEVELS = 60

C_MASS = 0.5
C_MOMENTUM = 0.8
FRIC_STEP = 0.5
LOAD_GAIN = 0.5
FLATHER = 0.7

ROWS = 120
COLS = 256
N_GX = 8
N_GY = 96
HELD = 4
PLAT = N_GY * N_GX * HELD
COL_PLAT = N_GY * HELD

HALO = 2 * SUBSTEPS
EXT = ROWS + 2 * HALO
WIDE = COLS + 128
GROUP = 48
FIELDS = 5
SPAN = FIELDS * HALO
CELL_ROW = GROUP
STRIP_ROW = GROUP + 9
SLOT_ROWS = 62
BACK_ROWS = 8
CHUNK = 512
FIRST_ROW = 68
FIRST_COL = 5
ROW_GROUP = [[(n + FIRST_ROW) % N_GY for n in range(N_GY)]]
COL_GROUP = [[(n + FIRST_COL) % N_GX for n in range(N_GX)]]
FIRST_BACK = 3
BACK_GROUP = [[(n + FIRST_BACK) % N_GX for n in range(N_GX)]]
PARTS = 2


def iota(shape, dim):
    return lax.broadcasted_iota(jnp.int32, shape, dim)


def row_slot(gy):
    return lax.rem(gy + (N_GY - FIRST_ROW), N_GY)


def col_slot(gx):
    gx = gx + (N_GX - FIRST_COL)
    return gx % N_GX if isinstance(gx, int) else lax.rem(gx, N_GX)


def three_parts(x):
    high = x.astype(jnp.bfloat16).astype(jnp.float32)
    rest = x - high
    middle = rest.astype(jnp.bfloat16).astype(jnp.float32)
    return [high, middle, rest - middle]


def decode(code):
    col = jnp.bitwise_and(code, COLS - 1)
    row = jnp.bitwise_and(jnp.right_shift(code, 8), 127)
    tile_x = jnp.bitwise_and(jnp.right_shift(code, 15), N_GX - 1)
    tile_y = jnp.right_shift(code, 18)
    return tile_y, tile_x, row, col


def column_of(row_vector):
    row_vector = jnp.concatenate([row_vector, jnp.zeros((1, 128 - ROWS), jnp.float32)], axis=1)
    return jnp.transpose(jnp.broadcast_to(row_vector, (128, 128)))


def fetch(pairs, sems):
    copies = [pltpu.make_async_copy(src, dst, sems.at[n]) for n, (src, dst) in enumerate(pairs)]
    for copy in copies:
        copy.start()
    return copies


def raw_kernel(drag_in, shear_in, strip_in, slots, drag, shear, strip, sems):
    pairs = ((drag_in, drag), (shear_in, shear), (strip_in, strip))
    for copy in fetch(pairs, sems):
        copy.wait()
    held = (drag[...], shear[0], shear[1])
    lines = []
    for t in range(6):
        pieces = []
        for h in range(2):
            i = 2 * (t % 2) + h
            pieces.append(held[t // 2][i : i + 1, :])
            pieces.append(strip[h, t // 2][t % 2 : t % 2 + 1, :])
        lines.append(jnp.concatenate(pieces, axis=1))
    block = jnp.concatenate(lines, axis=0)
    for j in range(N_GY):
        slots[j] = block


def row_halo_kernel(eta, flow_u, flow_v, friction, levels, smap, top, bottom):
    last = ROWS - HALO
    for f, ref in enumerate((eta, flow_u, flow_v, friction, levels)):
        part = slice(f * HALO, (f + 1) * HALO)
        top[part, :] = ref[:HALO, :].astype(jnp.float32)
        bottom[part, :] = ref[last:, :].astype(jnp.float32)
    column = column_of(smap[...].astype(jnp.float32))
    for half in (slice(0, 128), slice(128, 256)):
        top[FIELDS * HALO :, half] = column[:HALO]
        bottom[FIELDS * HALO :, half] = column[last:ROWS]


def extended(f, ref, up, down):
    part = slice(f * HALO, (f + 1) * HALO)
    return jnp.concatenate([up[part, :], ref[...].astype(jnp.float32), down[part, :]], axis=0)


def cell_kernel(code, *refs):
    *fields, up, down, slots = refs
    gy = lax.axis_index("gy")
    gx = lax.axis_index("gx")
    wide = [extended(f, ref, up, down) for f, ref in enumerate(fields)]
    stack = three_parts(wide[1]) + three_parts(wide[2]) + [wide[4]]
    stack.append(jnp.zeros((HALO, COLS), jnp.float32))
    table = jnp.concatenate(stack, axis=0).astype(jnp.bfloat16)
    for start in range(0, PLAT, CHUNK):
        tile_y, tile_x, row, col = decode(code[:, start : start + CHUNK])
        place = (tile_y - gy) * ROWS + row + HALO
        near = (tile_x == gx) & (place >= 0) & (place < EXT)
        hot = iota((COLS, CHUNK), 0) == jnp.where(near, col, -1)
        found = jnp.dot(
            table, hot.astype(jnp.bfloat16), preferred_element_type=jnp.float32
        )
        mine = iota((EXT, CHUNK), 0) == place
        parts = [found[n * EXT : (n + 1) * EXT] for n in range(7)]
        values = [
            parts[0] + parts[1] + parts[2],
            parts[3] + parts[4] + parts[5],
            parts[6],
        ]
        for f, value in enumerate(values):
            line = jnp.sum(jnp.where(mine, value, 0.0), axis=0, keepdims=True)
            for b in range(CHUNK // 128):
                block = start // 128 + b
                r = CELL_ROW + 3 * f + block % 3
                slots[col_slot(block // 3), r : r + 1, :] = line[:, b * 128 : (b + 1) * 128]
    lane = iota((GROUP, 128), 1)
    west = jnp.zeros((GROUP, 128), jnp.float32)
    east = jnp.zeros((GROUP, 128), jnp.float32)
    for f in range(FIELDS):
        tall = jnp.concatenate(
            [wide[f], jnp.zeros((3 * GROUP - EXT, COLS), jnp.float32)], axis=0
        )
        for g in range(3):
            at = g * SPAN + f * HALO
            rows = slice(g * GROUP, (g + 1) * GROUP)
            mask = (lane >= at) & (lane < at + HALO)
            moved = pltpu.roll(tall[rows, :128], at, 1)
            west = jnp.where(mask, moved, west)
            moved = pltpu.roll(tall[rows, 128:], (at + HALO) % 128, 1)
            east = jnp.where(mask, moved, east)
    for j in range(N_GX):
        slots[col_slot(j), :GROUP, :] = jnp.where(j > gx, east, west)
    for j in range(N_GX):
        slots[j, CELL_ROW + 9 :, :] = jnp.zeros((SLOT_ROWS - CELL_ROW - 9, 128), jnp.float32)


def strip_kernel(raw, slots_in, slots):
    gy = lax.axis_index("gy")
    blocks = [raw[row_slot(jnp.clip(gy - 2 + b, 0, N_GY - 1))] for b in range(5)]
    lane = iota((8, 128), 1)
    group = jnp.right_shift(jnp.bitwise_and(lane, 63), 2)
    strip = jnp.zeros((8, 128), jnp.float32)
    for t in range(6):
        lines = [block[t : t + 1, :] for block in blocks] + [jnp.zeros((3, 128), jnp.float32)]
        moved = pltpu.roll(jnp.concatenate(lines, axis=0), (4 * t - LEVELS) % 128, 1)
        strip = jnp.where(group == t, moved, strip)
    for j in range(N_GX):
        slots[j, STRIP_ROW : STRIP_ROW + 5, :] = strip[:5]


def load_kernel(cells, raw, slots):
    total = cells[0, CELL_ROW : CELL_ROW + 9, :]
    for j in range(1, N_GX):
        total = total + cells[j, CELL_ROW : CELL_ROW + 9, :]
    lines = []
    for f in range(3):
        line = jnp.concatenate([total[3 * f + q : 3 * f + q + 1, :] for q in range(3)], axis=1)
        for i in range(HELD):
            part = line[:, i * N_GY : (i + 1) * N_GY]
            lines.append(
                jnp.concatenate([part, jnp.zeros((1, 128 - N_GY), jnp.float32)], axis=1)
            )
    lines.append(jnp.zeros((128 - len(lines), 128), jnp.float32))
    columns = jnp.transpose(jnp.concatenate(lines, axis=0))[:N_GY]
    lane = iota((N_GY, 128), 1)
    low = lane < 64
    level = jnp.bitwise_and(lane, 63).astype(jnp.float32)
    result = jnp.zeros((N_GY, 128), jnp.float32)
    for q in range(2):
        u, v, wet = [
            jnp.where(
                low,
                columns[:, f * HELD + 2 * q : f * HELD + 2 * q + 1],
                columns[:, f * HELD + 2 * q + 1 : f * HELD + 2 * q + 2],
            )
            for f in range(3)
        ]
        depth = jnp.maximum(wet, 1.0) / LEVELS
        ux = u / depth + raw[:, 2 + q, :]
        uy = v / depth + raw[:, 4 + q, :]
        drag = jnp.where(level < wet, raw[:, q, :] * jnp.sqrt(ux * ux + uy * uy), 0.0)
        for c, flow in enumerate((ux, uy)):
            product = drag * flow
            for h in range(2):
                share = jnp.where(low, product, 0.0) if h == 0 else jnp.where(low, 0.0, product)
                load = jnp.sum(share, axis=1, keepdims=True) / LEVELS
                result = jnp.where(lane == c * HELD + 2 * q + h, load, result)
    result = jnp.concatenate([result, jnp.zeros((128 - N_GY, 128), jnp.float32)], axis=0)
    rows = jnp.transpose(result)
    out = []
    for c in range(2):
        line = jnp.concatenate(
            [rows[c * HELD + i : c * HELD + i + 1, :N_GY] for i in range(HELD)], axis=1
        )
        out += [line[:, q * 128 : (q + 1) * 128] for q in range(3)]
    out.append(jnp.zeros((2, 128), jnp.float32))
    block = jnp.concatenate(out, axis=0)
    for j in range(N_GX):
        slots[j] = block


def inside_of(gy, gx):
    row = iota((EXT, WIDE), 0)
    lane = iota((EXT, WIDE), 1)
    inside = ((row >= HALO) | (gy > 0)) & ((row < HALO + ROWS) | (gy < N_GY - 1))
    return inside & (
        (lane < COLS)
        | ((lane < COLS + HALO) & (gx < N_GX - 1))
        | ((lane >= WIDE - HALO) & (gx > 0))
    )


def half_step(e, u, v, rub, push, inside, emit=None):
    spread = pltpu.roll(u, WIDE - 1, 1) - pltpu.roll(u, 1, 1)
    spread = spread + (pltpu.roll(v, EXT - 1, 0) - pltpu.roll(v, 1, 0))
    mid = jnp.where(inside, e - C_MASS * spread, 0.0)
    if emit is not None:
        emit(0, mid)
    scale = 1.0 / (1.0 + rub * jnp.sqrt(u * u + v * v))
    slope_x = pltpu.roll(mid, WIDE - 1, 1) - pltpu.roll(mid, 1, 1)
    slope_y = pltpu.roll(mid, EXT - 1, 0) - pltpu.roll(mid, 1, 0)
    return mid, (u - push * slope_x) * scale, (v - push * slope_y) * scale, scale


def ready_for_steps(smap, cells, fields, up, down, gy, gx):
    from_west = cells[col_slot(jnp.maximum(gx - 1, 0)), :GROUP, :]
    from_east = cells[col_slot(jnp.minimum(gx + 1, N_GX - 1)), :GROUP, :]
    lane = iota((GROUP, 128), 1)

    def widened(f, ref):
        side = []
        for g in range(3):
            at = g * SPAN + f * HALO
            east = pltpu.roll(from_east, (-at) % 128, 1)
            west = pltpu.roll(from_west, (120 - at) % 128, 1)
            side.append(jnp.where(lane < HALO, east, jnp.where(lane >= 120, west, 0.0)))
        side = jnp.concatenate(side, axis=0)[:EXT]
        return jnp.concatenate([extended(f, ref, up, down), side], axis=1)

    e, u, v, fric, lev = [widened(f, ref) for f, ref in enumerate(fields)]
    inside = inside_of(gy, gx)
    e = jnp.where(inside, e, 0.0)
    u = jnp.where(inside, u, 0.0)
    v = jnp.where(inside, v, 0.0)
    depth = jnp.where(inside, lev / LEVELS, 1.0)
    rub = jnp.where(inside, FRIC_STEP * fric / (depth * depth), 1.0)
    push = C_MOMENTUM * depth
    mid, u, v, scale = half_step(e, u, v, rub, push, inside)
    ends = FIELDS * HALO
    ids = jnp.concatenate(
        [up[ends:, :128], column_of(smap[...].astype(jnp.float32))[:ROWS], down[ends:, :128]],
        axis=0,
    ).astype(jnp.int32)
    parents = jnp.concatenate(
        [cells[col_slot(j), STRIP_ROW : STRIP_ROW + 5, :] for j in range(N_GX)]
        + [jnp.zeros((128 - 5 * N_GX, 128), jnp.float32)],
        axis=0,
    )
    source = iota((EXT, 128), 1)
    column = jnp.zeros((EXT, 128), jnp.int32)
    for step in range(1, N_GX):
        column = column + (source >= 5 * step).astype(jnp.int32)
    first = ((gy - 2 + source - 5 * column) * N_GX + column) * 3
    slot_lane = jnp.right_shift(jnp.bitwise_and(iota((128, 128), 1), 63), 3)
    bound = jnp.zeros((EXT, 128), jnp.float32)
    for j in range(3):
        held = (ids == first + j) & (source < 5 * N_GX)
        for piece in three_parts(jnp.where(slot_lane == j, parents, 0.0)):
            bound = bound + jnp.dot(
                held.astype(jnp.bfloat16),
                piece.astype(jnp.bfloat16),
                preferred_element_type=jnp.float32,
            )
    bound = bound + pltpu.roll(bound, 120, 1) + pltpu.roll(bound, 112, 1)

    return mid, u, v, scale, rub, push, bound, inside


def step_kernel(smap, code, loads, cells, *refs):
    *fields, up, down, out_eta, out_u, out_v, force, fringe, staged, sems = refs
    outs = (out_eta, out_u, out_v)

    def send(n, field):
        staged[n] = field[HALO : HALO + ROWS, :COLS]
        pltpu.make_async_copy(staged.at[n], outs[n], sems.at[n]).start()

    gy = lax.axis_index("gy")
    gx = lax.axis_index("gx")
    for start in range(0, PLAT, CHUNK):
        tile_y, tile_x, row, col = decode(code[:, start : start + CHUNK])
        place = (tile_y - gy) * ROWS + row + HALO
        mine = iota((EXT, CHUNK), 0) == place
        across = (tile_x - gx) * COLS + col
        beside = jnp.where(across < 0, across + 2 * HALO, across - COLS)
        beside = jnp.where((across >= -HALO) & (across < COLS + HALO), beside, -1)
        right = (iota((COLS, CHUNK), 0) == across).astype(jnp.bfloat16)
        edge = iota((2 * HALO, CHUNK), 0) == beside
        left = []
        side = []
        for c in range(2):
            line = jnp.concatenate(
                [
                    loads[(b // 3 - FIRST_BACK) % N_GX, 3 * c + b % 3 : 3 * c + b % 3 + 1, :]
                    for b in range(start // 128, (start + CHUNK) // 128)
                ],
                axis=1,
            )
            for part in three_parts(line)[:PARTS]:
                left.append(jnp.where(mine, part, 0.0))
                side.append(jnp.where(edge, part, 0.0))
        side.append(jnp.zeros((128 - 2 * HALO * len(side), CHUNK), jnp.float32))
        left = jnp.concatenate(left, axis=0).astype(jnp.bfloat16)
        side = jnp.concatenate(side, axis=0).astype(jnp.bfloat16)
        dims = (((1,), (1,)), ((), ()))
        inner = lax.dot_general(left, right, dims, preferred_element_type=jnp.float32)
        outer = lax.dot_general(
            mine.astype(jnp.bfloat16), side, dims, preferred_element_type=jnp.float32
        )
        if start == 0:
            force[...] = inner
            fringe[...] = outer
        else:
            force[...] += inner
            fringe[...] += outer
    lane = iota((EXT, 128), 1)
    sides = fringe[...]
    forces = []
    for c in range(2):
        inner = force[c * PARTS * EXT : (c * PARTS + 1) * EXT, :]
        at = 2 * HALO * PARTS * c
        outer = pltpu.roll(sides, (-at) % 128, 1)
        for n in range(1, PARTS):
            inner = inner + force[(c * PARTS + n) * EXT : (c * PARTS + n + 1) * EXT, :]
            outer = outer + pltpu.roll(sides, (-at - 2 * HALO * n) % 128, 1)
        west = pltpu.roll(outer, 128 - 2 * HALO, 1)
        outer = jnp.where(lane < HALO, outer, jnp.where(lane >= 128 - HALO, west, 0.0))
        forces.append(LOAD_GAIN * jnp.concatenate([inner, outer], axis=1))
    force_x, force_y = forces

    mid, flow_u, flow_v, scale, rub, push, bound, inside = ready_for_steps(
        smap, cells, fields, up, down, gy, gx
    )
    side_lane = iota((EXT, 128), 1)
    at_west = (side_lane == 0) & (gx == 0)
    at_east = (side_lane == 127) & (gx == N_GX - 1)
    root = FLATHER * jnp.sqrt(push[:, :COLS] * (1.0 / C_MOMENTUM))

    def finish(step, mid, u, v):
        sea, flow = [bound[:, 4 * f + step : 4 * f + step + 1] for f in range(2)]
        west = flow - root[:, :128] * (mid[:, :128] - sea)
        sea, flow = [bound[:, 64 + 4 * f + step : 64 + 4 * f + step + 1] for f in range(2)]
        east = flow + root[:, 128:] * (mid[:, 128:COLS] - sea)
        u = jnp.concatenate(
            [
                jnp.where(at_west, west, u[:, :128]),
                jnp.where(at_east, east, u[:, 128:COLS]),
                u[:, COLS:],
            ],
            axis=1,
        )
        u = jnp.where(inside, u, 0.0)
        if step == SUBSTEPS - 1:
            send(1, u)
        return u, jnp.where(inside, v, 0.0)

    e = mid
    u, v = finish(0, e, flow_u - force_x * scale, flow_v - force_y * scale)
    for step in range(1, SUBSTEPS):
        emit = send if step == SUBSTEPS - 1 else None
        e, u, v, s = half_step(e, u, v, rub, push, inside, emit)
        u, v = finish(step, e, u - force_x * s, v - force_y * s)
    send(2, v)
    for n in range(3):
        pltpu.make_async_copy(staged.at[n], outs[n], sems.at[n]).wait()


def call(
    kernel, out_shape, spaces, name, scratch=(), limit=12, cycles=1, out_space=pltpu.VMEM, **kw
):
    many = isinstance(out_shape, list)
    out_spec = pl.BlockSpec(memory_space=out_space)
    return pl.pallas_call(
        kernel,
        out_shape=out_shape,
        in_specs=[pl.BlockSpec(memory_space=space) for space in spaces],
        out_specs=[out_spec] * len(out_shape) if many else out_spec,
        scratch_shapes=list(scratch),
        compiler_params=pltpu.CompilerParams(vmem_limit_bytes=limit * 1024 * 1024),
        cost_estimate=pl.CostEstimate(
            flops=cycles * 10**8, bytes_accessed=cycles * 2 * 10**6, transcendentals=0
        ),
        name=name,
        **kw,
    )


def f32(*shape):
    return jax.ShapeDtypeStruct(shape, jnp.float32)


def on_device(
    sea_level,
    transport_x,
    transport_y,
    friction,
    levels,
    strip_map,
    parent_strip,
    plat_tile,
    plat_row,
    plat_col,
    plat_drag,
    plat_shear,
):
    fields = (sea_level, transport_x, transport_y, friction, levels)
    smap = strip_map.reshape(1, ROWS)
    vmem, hbm = pltpu.VMEM, pltpu.HBM
    sems = pltpu.SemaphoreType.DMA

    held = call(
        raw_kernel,
        f32(N_GY, 6, 128),
        [hbm] * 3,
        "raw",
        [
            pltpu.VMEM((HELD, LEVELS), jnp.float32),
            pltpu.VMEM((2, HELD, LEVELS), jnp.float32),
            pltpu.VMEM((2, 3, 2, SUBSTEPS), jnp.float32),
            sems((3,)),
        ],
        60,
    )(plat_drag.T, plat_shear.transpose(0, 2, 1), parent_strip.transpose(0, 3, 2, 1))
    raw = lax.all_to_all(
        held, "gy", 0, 0, axis_index_groups=ROW_GROUP, tiled=True
    )

    top, bottom = call(
        row_halo_kernel, [f32(GROUP, COLS), f32(GROUP, COLS)], [vmem] * 6, "row_halo"
    )(*fields, smap)
    count = lax.axis_size("gy")
    upward = [(i, i + 1) for i in range(count - 1)]
    downward = [(target, source) for source, target in upward]
    near = (*fields, lax.ppermute(bottom, "gy", upward), lax.ppermute(top, "gy", downward))

    code = (plat_tile << 15) | (plat_row << 8) | plat_col
    start = FIRST_ROW * N_GX * HELD
    code = jnp.concatenate([code[start:], code[:start]]).reshape(N_GY, N_GX, HELD).transpose(1, 2, 0).reshape(1, PLAT)
    slots = call(
        cell_kernel,
        f32(N_GX, SLOT_ROWS, 128),
        [vmem] * 8,
        "cells",
        cycles=4,
    )(code, *near)
    slots = call(
        strip_kernel,
        f32(N_GX, SLOT_ROWS, 128),
        [vmem, vmem],
        "strips",
        input_output_aliases={1: 0},
    )(raw, slots)
    cells = lax.all_to_all(slots, "gx", 0, 0, axis_index_groups=COL_GROUP, tiled=True)
    slots = call(load_kernel, f32(N_GX, BACK_ROWS, 128), [vmem, vmem], "loads")(cells, raw)
    loads = lax.all_to_all(slots, "gx", 0, 0, axis_index_groups=BACK_GROUP, tiled=True)
    out = f32(ROWS, COLS)
    force = [
        pltpu.VMEM((2 * PARTS * EXT, COLS), jnp.float32),
        pltpu.VMEM((EXT, 128), jnp.float32),
        pltpu.VMEM((3, ROWS, COLS), jnp.float32),
        sems((3,)),
    ]
    return tuple(
        call(step_kernel, [out, out, out], [vmem] * 11, "steps", force, out_space=hbm)(
            smap, code, loads, cells, *near
        )
    )


def solution(mesh):
    return jax.shard_map(
        on_device,
        mesh=mesh,
        in_specs=(
            P("gy", "gx"),
            P("gy", "gx"),
            P("gy", "gx"),
            P("gy", "gx"),
            P("gy", "gx"),
            P("gy"),
            P(None, None, None, ("gy", "gx")),
            P(),
            P(),
            P(),
            P(None, ("gy", "gx")),
            P(None, None, ("gy", "gx")),
        ),
        out_specs=(P("gy", "gx"), P("gy", "gx"), P("gy", "gx")),
        check_vma=False,
    )
```
